128 devices in a mesh: gx: 8 (over x_lo, y), gy: 16 (over x_hi, z, core).
Axes of the slice: x: 4 (x_hi: 2, x_lo: 2; x = x_hi * 2 + x_lo), y: 4, z: 4, core: 2. Of those that a mesh axis runs over, the one named last changes fastest.
Arguments:
- coefficients: bfloat16 [16, 8, 256, 2048], P('gy', 'gx'), may hold values from -6 to 6
- src_blocks: bfloat16 [4, 16, 2, 2, 32, 32], replicated, may hold values from -0.5 to 0.5
- mid_blocks: bfloat16 [16, 2, 32, 32], replicated, may hold values from -0.75 to 0.75
- obs_blocks: bfloat16 [4, 16, 2, 2, 32, 32], replicated, may hold values from -0.5 to 0.5
- block_ids: int32 [16, 8, 256, 9], P('gy', 'gx'), may hold values from 0 to 15
- partner_perm: int32 [8, 256], replicated, may hold values from 0 to 255, each once within a row
- owner_order: int32 [16, 8, 256], P('gy', 'gx'), may hold values from 0 to 255, each once within a row
Outputs:
- field_coeffs: bfloat16 [16, 8, 256, 2048], P('gy', 'gx')
The draws below stay inside these ranges and needn't reach their ends.
Inputs may be any that keep to these rules, and one draw needn't show every extreme that they name: `partner_perm`: each row is a permutation. `owner_order`: each device's row is a permutation.
All inputs are finite; a program needn't handle non-finite values.
Results may differ from the reference program's by a relative error of at most 0.019.
Values may be sent and summed in bfloat16 or wider, within the bound.
No kernel may reach another device: no remote copies, remote signals or barrier semaphores. Data moves between devices by JAX's collectives and lax.ppermute only.
A program may use at most 64 MiB of HBM per device.

```python
import jax
import jax.numpy as jnp
from jax import lax

RANK = 32
RHS = 32
CLUSTERS = 256
LEVELS = 4
KINDS = 16
FEAT = 2048
N_GX = 8
N_GY = 16


def place_ends(values, key, least, largest):
    place = [jax.random.randint(jax.random.fold_in(key, axis), (), 0, length) for axis, length in enumerate(values.shape)]
    widest = values.shape.index(max(values.shape))
    next_to = place[:widest] + [(place[widest] + 1) % values.shape[widest]] + place[widest + 1:]
    return values.at[tuple(place)].set(least).at[tuple(next_to)].set(largest)


def level_of(key, dims, shards, least, high):
    def one(axis_at, parts):
        steps = jax.random.uniform(jax.random.fold_in(jax.random.fold_in(key, 6), axis_at), (parts,), jnp.float32, least / len(shards), high / len(shards))
        return jnp.repeat(jnp.exp(steps), dims[axis_at] // parts).reshape((-1,) + (1,) * (len(dims) - axis_at - 1))

    loudness = one(*shards[0])
    for cut in shards[1:]:
        loudness = loudness * one(*cut)
    return loudness


def noise(rng, dims, width, bound, shards=(), held_as=jnp.bfloat16):
    level = level_of(rng, dims, shards, -0.22, 0.18) if shards else 1.0
    values = jax.random.normal(rng, dims, jnp.float32) * width * level
    return jnp.minimum(jnp.maximum(values, -bound), bound).astype(held_as)


def setup_inputs(seed: int = 0) -> dict:
    streams_of = jax.random.split(jax.random.key(seed), 8)
    coefficients = noise(streams_of[0], (N_GY, N_GX, CLUSTERS, FEAT), 1.0, 6.0, ((0, 16), (1, 8)))
    src_blocks = noise(streams_of[1], (LEVELS, KINDS, 2, 2, RANK, RANK), (4 * RANK) ** -0.5, 0.5)
    mid_blocks = noise(streams_of[2], (KINDS, 2, RANK, RANK), (2 * RANK) ** -0.5, 0.75)
    obs_blocks = noise(streams_of[3], (LEVELS, KINDS, 2, 2, RANK, RANK), (4 * RANK) ** -0.5, 0.5)
    block_ids = place_ends(jax.random.randint(streams_of[4], (N_GY, N_GX, CLUSTERS, 2 * LEVELS + 1), 0, KINDS), jax.random.fold_in(streams_of[4], 1), 0, KINDS - 1).astype(jnp.int32)
    partner_perm = jax.vmap(lambda own: jax.random.permutation(own, CLUSTERS))(jax.random.split(streams_of[5], (2 * LEVELS))).reshape((2 * LEVELS, CLUSTERS)).astype(jnp.int32)
    owner_order = jax.vmap(lambda own: jax.random.permutation(own, CLUSTERS))(jax.random.split(streams_of[6], N_GY * N_GX)).reshape((N_GY, N_GX, CLUSTERS)).astype(jnp.int32)
    return dict(coefficients=coefficients, src_blocks=src_blocks, mid_blocks=mid_blocks, obs_blocks=obs_blocks, block_ids=block_ids, partner_perm=partner_perm, owner_order=owner_order)


def real_form(blocks):
    real_part = jnp.swapaxes(blocks[..., 0, :, :], -1, -2)
    imag_part = jnp.swapaxes(blocks[..., 1, :, :], -1, -2)
    upper_rows = jnp.concatenate([real_part, imag_part], -1)
    lower_rows = jnp.concatenate([-imag_part, real_part], -1)
    return jnp.concatenate([upper_rows, lower_rows], -2)


def apply_blocks(values, kinds, table):
    weights = table[kinds].astype(jnp.float32)
    shaped = values.astype(jnp.float32).reshape(CLUSTERS, RHS, 2 * RANK)
    return jnp.einsum('csr,crt->cst', shaped, weights)


def butterfly_level(current, kind_column, perm_row, own_table, far_table, tree_bit, device_count):
    def per_device(device):
        partner = current[jnp.bitwise_xor(device, 1 << tree_bit)][perm_row]
        kinds = kind_column[device]
        summed = apply_blocks(current[device], kinds, own_table) + apply_blocks(partner, kinds, far_table)
        return summed.astype(jnp.bfloat16).reshape(CLUSTERS, FEAT)
    return lax.map(per_device, jnp.arange(device_count, dtype=jnp.int32))


def reference(coefficients, src_blocks, mid_blocks, obs_blocks, block_ids, partner_perm, owner_order):
    device_count = N_GX * N_GY
    tree_depth = device_count.bit_length() - 1
    current = coefficients.reshape(device_count, CLUSTERS, FEAT)
    kind_table = block_ids.reshape(device_count, CLUSTERS, 2 * LEVELS + 1)
    src_table = real_form(src_blocks)
    obs_table = real_form(obs_blocks)
    mid_table = real_form(mid_blocks)
    for level in range(LEVELS):
        current = butterfly_level(current, kind_table[:, :, level], partner_perm[level],
                                  src_table[level, :, 0], src_table[level, :, 1], level, device_count)
    send_order = owner_order.reshape(device_count, CLUSTERS)
    current = jnp.take_along_axis(current, send_order[:, :, None], 1)
    slot_count = CLUSTERS // device_count
    moved = current.reshape(N_GY, N_GX, CLUSTERS, FEAT).transpose(1, 0, 2, 3)
    moved = moved.reshape(device_count, device_count, slot_count, FEAT).transpose(1, 0, 2, 3)
    moved = moved.reshape(N_GX, N_GY, CLUSTERS, FEAT).transpose(1, 0, 2, 3)
    current = moved.reshape(device_count, CLUSTERS, FEAT)

    def middle(device):
        summed = apply_blocks(current[device], kind_table[device, :, LEVELS], mid_table)
        return summed.astype(jnp.bfloat16).reshape(CLUSTERS, FEAT)
    current = lax.map(middle, jnp.arange(device_count, dtype=jnp.int32))
    for level in range(LEVELS):
        current = butterfly_level(current, kind_table[:, :, LEVELS + 1 + level], partner_perm[LEVELS + level],
                                  obs_table[level, :, 0], obs_table[level, :, 1],
                                  tree_depth - 1 - level, device_count)
    return current.reshape(N_GY, N_GX, CLUSTERS, FEAT)
```

```python
import functools

import jax
import jax.numpy as jnp
import numpy as np
from jax import lax
from jax.experimental import pallas as pl
from jax.experimental.pallas import tpu as pltpu
from jax.sharding import PartitionSpec as P

NA = 8
MEMBERS = 16
CLUSTERS = 256
LANES = 128
HALF = 64
IDS = 16
EXTRA = 2 * IDS
AXES = ("gx", "gy")
BF = jnp.bfloat16
F32 = jnp.float32


def number(a, b, c):
    return 16 * a + 2 * b + c


SRC_GROUPS = [[number((t // 2) ^ b, b, t % 2) for t in range(MEMBERS)] for b in range(NA)]
MID_GROUPS = [[number(a, r ^ a, c) for a in range(NA)] for r in range(NA) for c in range(2)]
OBS_GROUPS = [[number(a, (t // 2) ^ a, t % 2) for t in range(MEMBERS)] for a in range(NA)]


def position_order():
    row = np.arange(CLUSTERS)
    b, q, r, c = row >> 5, (row >> 4) & 1, (row >> 1) & 7, row & 1
    return ((r ^ b) * 16 + b * 2 + c) * 2 + q


ORDER = position_order()


def pack_kernel(coef_ref, ids_ref, send_ref, ordered_ref, out_ref):
    ids = jnp.concatenate([ids_ref[...].astype(F32), jnp.zeros((CLUSTERS, LANES - 9), F32)], axis=1).T[:MEMBERS]
    ordered = jnp.dot(ids.astype(BF), ordered_ref[...], preferred_element_type=F32)
    pad = jnp.zeros((3, CLUSTERS), F32)
    source = jnp.concatenate([ids[:4], send_ref[...].astype(F32), pad], axis=0)
    other = jnp.concatenate([ordered[4:8], ids[8:9], pad], axis=0)
    extra = jnp.concatenate([source[:, :LANES], source[:, LANES:], other[:, :LANES], other[:, LANES:]], axis=0)
    extra = extra.astype(BF)
    for t in range(MEMBERS):
        out_ref[t, :CLUSTERS, :] = coef_ref[:, t * LANES : (t + 1) * LANES]
        out_ref[t, CLUSTERS:, :] = extra


def turned_weights(block, parts):
    rows = []
    for low in range(4):
        each = [(4 * high + low, part) for high in range(4) for part in range(parts)]
        top = [(block(k, p, 0), -block(k, p, 1)) for k, p in each]
        bottom = [(block(k, p, 1), block(k, p, 0)) for k, p in each]
        rows += [jnp.concatenate([piece for pair in half for piece in pair], axis=1) for half in (top, bottom)]
    return jnp.concatenate(rows, axis=0).T.astype(BF)


def table_kernel(
    src_ref, mid_ref, obs_ref, perm_ref, ordered_ref, order_ref,
    src_perm_ref, obs_perm_ref, src_w_ref, obs_w_ref, mid_w_ref,
):
    perm = perm_ref[...].astype(F32)
    moved = jnp.dot(perm.astype(BF), ordered_ref[...], preferred_element_type=F32)
    turned = jnp.concatenate([perm, moved, jnp.zeros((LANES - 16, CLUSTERS), F32)], axis=0).T
    shape = (CLUSTERS, CLUSTERS)
    count = lax.broadcasted_iota(jnp.int32, shape, 1).astype(F32)
    order = jnp.broadcast_to(order_ref[...], shape)

    def match(column, against):
        return jnp.where(jnp.broadcast_to(column, shape) == against, 1.0, 0.0).astype(BF)

    for l in range(4):
        src_perm_ref[l] = match(turned[:, l : l + 1], count)
        at = 12 + l if l < 3 else 7
        obs_perm_ref[l] = match(turned[:, at : at + 1], order)
    obs_perm_ref[4] = match(lax.broadcasted_iota(jnp.int32, shape, 0).astype(F32), order)

    def weights(l, carry):
        src_w_ref[l] = turned_weights(lambda k, p, i: src_ref[l, k, p, i].astype(F32), 2)
        obs_w_ref[l] = turned_weights(lambda k, p, i: obs_ref[l, k, p, i].astype(F32), 2)
        return carry

    lax.fori_loop(0, 4, weights, 0)
    mid_w_ref[...] = turned_weights(lambda k, p, i: mid_ref[k, i].astype(F32), 1)


def spread_kinds(kt_ref, kb_ref, row):
    for m in range(MEMBERS):
        for half in range(2):
            col = m * IDS + 8 * half + row
            kinds = jnp.broadcast_to(kt_ref[:, col : col + 1], (LANES, LANES))
            high = jnp.floor(kinds * 0.25)
            at = slice(half * LANES, (half + 1) * LANES)
            kb_ref[0, m, at, :] = high.astype(BF)
            kb_ref[1, m, at, :] = (kinds - 4.0 * high).astype(BF)


def swap_halves(x):
    return jnp.concatenate([x[:, HALF:], x[:, :HALF]], axis=1)


def low_lanes():
    return lax.broadcasted_iota(jnp.int32, (CLUSTERS, LANES), 1) < HALF


def choose(prod_u, prod_v, low):
    second = low >= 2.0
    odd = (low == 1.0) | (low == 3.0)
    fu = jnp.where(second, prod_u[:, LANES:].astype(BF), prod_u[:, :LANES].astype(BF))
    fv = jnp.where(second, prod_v[:, LANES:].astype(BF), prod_v[:, :LANES].astype(BF))
    left = jnp.where(odd, swap_halves(fu), fu)
    right = jnp.where(odd, fv, swap_halves(fv))
    return jnp.concatenate([left[:, :HALF], right[:, HALF:]], axis=1)


def expand(x, high):
    zero = jnp.zeros_like(x)
    return jnp.concatenate([jnp.where(high == float(j), x, zero) for j in range(4)], axis=1)


def level(read, write, perm, weights, kb_ref, mask, own_perm=None):
    def body(i, carry):
        ms = [2 * i, 2 * i + 1]
        far = jnp.concatenate([read(m ^ mask) for m in ms], axis=1)
        far = jnp.dot(perm, far, preferred_element_type=F32).astype(BF)
        own = jnp.concatenate([read(m) for m in ms], axis=1)
        if own_perm is not None:
            own = jnp.dot(own_perm, own, preferred_element_type=F32).astype(BF)
        rows = []
        for k, m in enumerate(ms):
            x = own[:, k * LANES : (k + 1) * LANES]
            y = far[:, k * LANES : (k + 1) * LANES]
            high = kb_ref[0, m]
            rows.append(expand(jnp.concatenate([x[:, :HALF], y[:, :HALF]], axis=1), high))
            rows.append(expand(jnp.concatenate([x[:, HALF:], y[:, HALF:]], axis=1), high))
        prod = jnp.dot(jnp.concatenate(rows, axis=0), weights[...], preferred_element_type=F32)
        for k, m in enumerate(ms):
            at = 2 * k * CLUSTERS
            write(m, choose(prod[at : at + CLUSTERS], prod[at + CLUSTERS : at + 2 * CLUSTERS], kb_ref[1, m]))
        return carry

    lax.fori_loop(0, MEMBERS // 2, body, 0)


def source_kernel(place_ref, x_ref, perm_ref, w_ref, out_ref, kt_ref, kb_ref, s_ref, f_ref):
    b = place_ref[0]
    kt_ref[...] = x_ref[:, CLUSTERS : CLUSTERS + IDS, :].reshape(MEMBERS * IDS, LANES).astype(F32).T
    for l, mask in enumerate((2, 4, 8, 1)):
        spread_kinds(kt_ref, kb_ref, l)

        def read(m, l=l):
            return x_ref[m, :CLUSTERS, :] if l == 0 else s_ref[(l - 1) % 2, m]

        def write(m, value, l=l):
            s_ref[l % 2, m] = value

        level(read, write, perm_ref[l], w_ref.at[l], kb_ref, mask)
    lane = lax.broadcasted_iota(jnp.int32, (LANES, LANES), 1).astype(F32)
    for m in range(MEMBERS):
        picks = []
        for half in range(2):
            col = m * IDS + 8 * half + 4
            at = jnp.broadcast_to(kt_ref[:, col : col + 1], (LANES, LANES))
            picks.append(
                jnp.concatenate([(at == lane).astype(F32), (at == lane + LANES).astype(F32)], axis=1).astype(BF)
            )
        sent = jnp.dot(jnp.concatenate(picks, axis=0), s_ref[1, m], preferred_element_type=F32)
        f_ref[m * CLUSTERS : (m + 1) * CLUSTERS, :] = sent
    for h in range(NA):
        for n in range(MEMBERS):
            slot = (h * MEMBERS + (n ^ (2 * h))) * 2
            parts = [
                f_ref[pl.ds(m0 * CLUSTERS + slot + q, 8, stride=CLUSTERS), :] for q in range(2) for m0 in (0, 8)
            ]
            out_ref[h, n * EXTRA : (n + 1) * EXTRA, :] = jnp.concatenate(parts, axis=0).astype(BF)
        for c in range(2):
            at = MEMBERS * EXTRA + c * IDS
            out_ref[h, at : at + IDS, :] = x_ref[(h ^ b) * 2 + c, CLUSTERS + IDS :, :]


def observation_kernel(place_ref, r_ref, perm_ref, w_ref, wmid_ref, out_ref, kt_ref, kb_ref, s_ref):
    b, diag = place_ref[0], place_ref[1]
    ids = [r_ref[(n // 2) ^ b, pl.ds(MEMBERS * EXTRA + (n % 2) * IDS, IDS), :] for n in range(MEMBERS)]
    kt_ref[...] = jnp.concatenate(ids, axis=0).astype(F32).T
    spread_kinds(kt_ref, kb_ref, 0)

    def middle(n, carry):
        x = jnp.concatenate([r_ref[i ^ diag, pl.ds(pl.multiple_of(n * EXTRA, EXTRA), EXTRA), :] for i in range(NA)], axis=0)
        high = kb_ref[0, n]
        other = swap_halves(x)
        low = low_lanes()
        zero = jnp.zeros_like(x)
        rows = []
        for doubled in (jnp.where(low, x, other), jnp.where(low, other, x)):
            parts = []
            for j in (0, 2):
                first = jnp.where(high == float(j), doubled, zero)
                later = jnp.where(high == float(j + 1), doubled, zero)
                parts.append(jnp.where(low, first, later))
            rows.append(jnp.concatenate(parts, axis=1))
        prod = jnp.dot(jnp.concatenate(rows, axis=0), wmid_ref[...], preferred_element_type=F32)
        s_ref[1, n] = choose(prod[:CLUSTERS], prod[CLUSTERS:], kb_ref[1, n])
        return carry

    lax.fori_loop(0, MEMBERS, middle, 0)
    for l, mask in enumerate((8, 4, 2, 1)):
        spread_kinds(kt_ref, kb_ref, l + 1)

        def read(n, l=l):
            return s_ref[(l + 1) % 2, n]

        def write(n, value, l=l):
            if l == 3:
                out_ref[n] = value
            else:
                s_ref[l % 2, n] = value

        level(read, write, perm_ref[l], w_ref.at[l], kb_ref, mask, perm_ref[4] if l == 3 else None)


VMEM = pl.BlockSpec(memory_space=pltpu.VMEM)
SMEM = pl.BlockSpec(memory_space=pltpu.SMEM)
LIMIT = 40 * 1024 * 1024


def call(kernel, name, out_shape, in_specs, scratch=(), flops=0, count=0):
    many = isinstance(out_shape, tuple)
    return pl.pallas_call(
        kernel,
        out_shape=out_shape,
        in_specs=in_specs,
        out_specs=(VMEM,) * len(out_shape) if many else VMEM,
        scratch_shapes=list(scratch),
        compiler_params=pltpu.CompilerParams(vmem_limit_bytes=LIMIT),
        cost_estimate=pl.CostEstimate(flops=flops, bytes_accessed=count, transcendentals=0),
        name=name,
    )


def on_device(coefficients, src_blocks, mid_blocks, obs_blocks, block_ids, partner_perm, owner_order):
    a = lax.axis_index("gx")
    b = lax.axis_index("gy") // 2
    place = jnp.stack([b, a ^ b]).astype(jnp.int32)
    ordered = jnp.asarray(np.eye(CLUSTERS)[:, ORDER], BF)
    order = jnp.asarray(ORDER[None], F32)

    def shape(*dims):
        return jax.ShapeDtypeStruct(dims, BF)

    x = call(pack_kernel, "pack", shape(MEMBERS, CLUSTERS + EXTRA, LANES), [VMEM] * 4, count=2**21)(
        coefficients[0, 0], block_ids[0, 0], owner_order[0], ordered
    )
    x = lax.all_to_all(x, AXES, split_axis=0, concat_axis=0, tiled=True, axis_index_groups=SRC_GROUPS)
    square, wide = (CLUSTERS, CLUSTERS), (8 * HALF, 4 * HALF)
    src_perm, obs_perm, src_w, obs_w, mid_w = call(
        table_kernel,
        "tables",
        (shape(4, *square), shape(5, *square), shape(4, *wide), shape(4, *wide), shape(4 * HALF, 4 * HALF)),
        [VMEM] * 6,
        flops=10**9,
        count=2**24,
    )(src_blocks, mid_blocks, obs_blocks, partner_perm, ordered, order)

    ids = pltpu.VMEM((LANES, MEMBERS * IDS), F32)
    state = pltpu.VMEM((2, MEMBERS, CLUSTERS, LANES), BF)
    mid = call(
        source_kernel,
        "source_levels",
        shape(NA, (MEMBERS + 1) * EXTRA, LANES),
        [SMEM, VMEM, VMEM, VMEM],
        (ids, state, state, pltpu.VMEM((MEMBERS * CLUSTERS, LANES), F32)),
    )(place, x, src_perm, src_w)
    mid = lax.all_to_all(mid, AXES, split_axis=0, concat_axis=0, tiled=True, axis_index_groups=MID_GROUPS)
    done = call(
        observation_kernel,
        "observation_levels",
        shape(MEMBERS, CLUSTERS, LANES),
        [SMEM, VMEM, VMEM, VMEM, VMEM],
        (ids, state, state),
    )(place, mid, obs_perm, obs_w, mid_w)
    out = lax.all_to_all(
        done.reshape(MEMBERS * CLUSTERS, LANES),
        AXES,
        split_axis=0,
        concat_axis=1,
        tiled=True,
        axis_index_groups=OBS_GROUPS,
    )
    return out.reshape(1, 1, CLUSTERS, MEMBERS * LANES)


def solution(mesh):
    in_specs = (
        P("gy", "gx", None, None),
        P(),
        P(),
        P(),
        P("gy", "gx", None, None),
        P(),
        P("gy", "gx", None),
    )
    out_specs = P("gy", "gx", None, None)
    return jax.shard_map(on_device, mesh=mesh, in_specs=in_specs, out_specs=out_specs, check_vma=False)
```

```python
import functools

import jax
import jax.numpy as jnp
import numpy as np
from jax import lax
from jax.experimental import pallas as pl
from jax.experimental.pallas import tpu as pltpu
from jax.sharding import PartitionSpec as P

NA = 8
MEMBERS = 16
CLUSTERS = 256
LANES = 128
HALF = 64
IDS = 16
EXTRA = 2 * IDS
AXES = ("gx", "gy")
BF = jnp.bfloat16
F32 = jnp.float32


def number(a, b, c):
    return 16 * a + 2 * b + c


SRC_GROUPS = [[number((t // 2) ^ b, b, t % 2) for t in range(MEMBERS)] for b in range(NA)]
MID_GROUPS = [[number(a, r ^ a, c) for a in range(NA)] for r in range(NA) for c in range(2)]
OBS_GROUPS = [[number(a, (t // 2) ^ a, t % 2) for t in range(MEMBERS)] for a in range(NA)]


def position_order():
    row = np.arange(CLUSTERS)
    b, q, r, c = row >> 5, (row >> 4) & 1, (row >> 1) & 7, row & 1
    return ((r ^ b) * 16 + b * 2 + c) * 2 + q


ORDER = position_order()


def pack_kernel(coef_ref, ids_ref, send_ref, ordered_ref, out_ref):
    ids = jnp.concatenate([ids_ref[...].astype(F32), jnp.zeros((CLUSTERS, LANES - 9), F32)], axis=1).T[:MEMBERS]
    ordered = jnp.dot(ids.astype(BF), ordered_ref[...], preferred_element_type=F32)
    pad = jnp.zeros((3, CLUSTERS), F32)
    source = jnp.concatenate([ids[:4], send_ref[...].astype(F32), pad], axis=0)
    other = jnp.concatenate([ordered[4:8], ids[8:9], pad], axis=0)
    extra = jnp.concatenate([source[:, :LANES], source[:, LANES:], other[:, :LANES], other[:, LANES:]], axis=0)
    extra = extra.astype(BF)
    for t in range(MEMBERS):
        out_ref[t, :CLUSTERS, :] = coef_ref[:, t * LANES : (t + 1) * LANES]
        out_ref[t, CLUSTERS:, :] = extra


def turned_weights(block, parts, lows):
    rows = []
    for low in lows:
        each = [(4 * high + low, part) for high in range(4) for part in parts]
        top = [(block(k, p, 0), -block(k, p, 1)) for k, p in each]
        bottom = [(block(k, p, 1), block(k, p, 0)) for k, p in each]
        rows += [jnp.concatenate([piece for pair in half for piece in pair], axis=1) for half in (top, bottom)]
    return jnp.concatenate(rows, axis=0).T.astype(BF)


FORMS = (((0, 1), (0, 1, 2, 3)), ((1, 0), (1, 0, 3, 2)))


def table_kernel(
    src_ref, mid_ref, obs_ref, perm_ref, ordered_ref, order_ref,
    src_perm_ref, obs_perm_ref, src_w_ref, obs_w_ref, mid_w_ref,
):
    perm = perm_ref[...].astype(F32)
    moved = jnp.dot(perm.astype(BF), ordered_ref[...], preferred_element_type=F32)
    turned = jnp.concatenate([perm, moved, jnp.zeros((LANES - 16, CLUSTERS), F32)], axis=0).T
    shape = (CLUSTERS, CLUSTERS)
    count = lax.broadcasted_iota(jnp.int32, shape, 1).astype(F32)
    order = jnp.broadcast_to(order_ref[...], shape)

    def match(column, against):
        return jnp.where(jnp.broadcast_to(column, shape) == against, 1.0, 0.0).astype(BF)

    for l in range(4):
        src_perm_ref[l] = match(turned[:, l : l + 1], count)
        at = 12 + l if l < 3 else 7
        obs_perm_ref[l] = match(turned[:, at : at + 1], order)
    obs_perm_ref[4] = match(lax.broadcasted_iota(jnp.int32, shape, 0).astype(F32), order)

    def weights(l, carry):
        for form, (parts, lows) in enumerate(FORMS):
            src_w_ref[l, form] = turned_weights(lambda k, p, i: src_ref[l, k, p, i].astype(F32), parts, lows)
            obs_w_ref[l, form] = turned_weights(lambda k, p, i: obs_ref[l, k, p, i].astype(F32), parts, lows)
        return carry

    lax.fori_loop(0, 4, weights, 0)
    for form, (_, lows) in enumerate(FORMS):
        mid_w_ref[form] = turned_weights(lambda k, p, i: mid_ref[k, i].astype(F32), (0,), lows)


def spread_kinds(kt_ref, kb_ref, row):
    for m in range(MEMBERS):
        for half in range(2):
            col = m * IDS + 8 * half + row
            kinds = jnp.broadcast_to(kt_ref[:, col : col + 1], (LANES, LANES))
            high = jnp.floor(kinds * 0.25)
            low = kinds - 4.0 * high
            second = jnp.floor(low * 0.5)
            at = slice(half * LANES, (half + 1) * LANES)
            kb_ref[0, m, at, :] = high.astype(BF)
            kb_ref[1, m, at, :] = second.astype(BF)
            kb_ref[2, m, at, :] = (low - 2.0 * second).astype(BF)


def first_side():
    return lax.broadcasted_iota(jnp.int32, (CLUSTERS, LANES), 1).astype(F32).astype(BF) < HALF


def other_side(x):
    return pltpu.roll(x, HALF, 1)


def expand(x, high):
    zero = jnp.zeros_like(x)
    return jnp.concatenate([jnp.where(high == float(j), x, zero) for j in range(4)], axis=1)


def expand_halves(x, high, first):
    zero = jnp.zeros_like(x)
    parts = []
    for j in (0, 2):
        parts.append(jnp.where(first, jnp.where(high == float(j), x, zero), jnp.where(high == float(j + 1), x, zero)))
    return jnp.concatenate(parts, axis=1)


def multiply(ms, rows, weights, kb_ref, write, first):
    prods = [
        jnp.dot(jnp.concatenate([r[side] for r in rows], axis=0), weights[side], preferred_element_type=F32)
        for side in range(2)
    ]
    for k, m in enumerate(ms):
        second, odd = kb_ref[1, m] > 0.5, kb_ref[2, m] > 0.5
        at = slice(k * CLUSTERS, (k + 1) * CLUSTERS)
        one, two = [jnp.where(second, p[at, LANES:].astype(BF), p[at, :LANES].astype(BF)) for p in prods]
        kept = jnp.where(jnp.logical_xor(first, odd), one, two)
        turned = other_side(kept)
        write(m, jnp.where(odd, turned, kept), jnp.where(odd, kept, turned))


BATCH = 8


def level(read, read_turned, write, perm, weights, kb_ref, mask, own_perm=None):
    def body(i, carry):
        first = first_side()
        ms = [BATCH * i + k for k in range(BATCH)]
        far = jnp.concatenate([read_turned(m ^ mask) for m in ms], axis=1)
        far = jnp.dot(perm, far, preferred_element_type=F32).astype(BF)
        own = [read(m) for m in ms]
        if own_perm is not None:
            own = jnp.dot(own_perm, jnp.concatenate(own, axis=1), preferred_element_type=F32).astype(BF)
            own = [own[:, k * LANES : (k + 1) * LANES] for k in range(BATCH)]
        rows = []
        for k, m in enumerate(ms):
            x, y, high = own[k], far[:, k * LANES : (k + 1) * LANES], kb_ref[0, m]
            rows.append((expand(jnp.where(first, x, y), high), expand(jnp.where(first, y, x), high)))
        multiply(ms, rows, weights, kb_ref, write, first)
        return carry

    lax.fori_loop(0, MEMBERS // BATCH, body, 0)


def source_kernel(place_ref, x_ref, perm_ref, w_ref, out_ref, kt_ref, kb_ref, s_ref, t_ref, f_ref):
    b = place_ref[0]
    kt_ref[...] = x_ref[:, CLUSTERS : CLUSTERS + IDS, :].reshape(MEMBERS * IDS, LANES).astype(F32).T
    for l, mask in enumerate((2, 4, 8, 1)):
        spread_kinds(kt_ref, kb_ref, l)

        def read(m, l=l):
            return x_ref[m, :CLUSTERS, :] if l == 0 else s_ref[(l - 1) % 2, m]

        def read_turned(m, l=l):
            return other_side(x_ref[m, :CLUSTERS, :]) if l == 0 else t_ref[(l - 1) % 2, m]

        def write(m, value, turned, l=l):
            s_ref[l % 2, m] = value
            t_ref[l % 2, m] = turned

        level(read, read_turned, write, perm_ref[l], w_ref.at[l], kb_ref, mask)
    lane = lax.broadcasted_iota(jnp.int32, (LANES, LANES), 1).astype(F32)
    for m in range(MEMBERS):
        picks = []
        for half in range(2):
            col = m * IDS + 8 * half + 4
            at = jnp.broadcast_to(kt_ref[:, col : col + 1], (LANES, LANES))
            picks.append(
                jnp.concatenate([(at == lane).astype(F32), (at == lane + LANES).astype(F32)], axis=1).astype(BF)
            )
        sent = jnp.dot(jnp.concatenate(picks, axis=0), s_ref[1, m], preferred_element_type=F32)
        f_ref[m * CLUSTERS : (m + 1) * CLUSTERS, :] = sent
    for h in range(NA):
        for n in range(MEMBERS):
            slot = (h * MEMBERS + (n ^ (2 * h))) * 2
            parts = [
                f_ref[pl.ds(m0 * CLUSTERS + slot + q, 8, stride=CLUSTERS), :] for q in range(2) for m0 in (0, 8)
            ]
            out_ref[h, n * EXTRA : (n + 1) * EXTRA, :] = jnp.concatenate(parts, axis=0).astype(BF)
        for c in range(2):
            at = MEMBERS * EXTRA + c * IDS
            out_ref[h, at : at + IDS, :] = x_ref[(h ^ b) * 2 + c, CLUSTERS + IDS :, :]


def observation_kernel(place_ref, r_ref, perm_ref, w_ref, wmid_ref, out_ref, kt_ref, kb_ref, s_ref, t_ref):
    b, diag = place_ref[0], place_ref[1]
    ids = [r_ref[(n // 2) ^ b, pl.ds(MEMBERS * EXTRA + (n % 2) * IDS, IDS), :] for n in range(MEMBERS)]
    kt_ref[...] = jnp.concatenate(ids, axis=0).astype(F32).T
    spread_kinds(kt_ref, kb_ref, 0)

    def put(slot):
        def write(n, value, turned):
            s_ref[slot, n] = value
            t_ref[slot, n] = turned

        return write

    def middle(i, carry):
        first = first_side()
        ns = [BATCH * i + k for k in range(BATCH)]
        rows = []
        for n in ns:
            at = pl.ds(pl.multiple_of(n * EXTRA, EXTRA), EXTRA)
            x = jnp.concatenate([r_ref[j ^ diag, at, :] for j in range(NA)], axis=0)
            turned, high = other_side(x), kb_ref[0, n]
            one, two = jnp.where(first, x, turned), jnp.where(first, turned, x)
            rows.append((expand_halves(one, high, first), expand_halves(two, high, first)))
        multiply(ns, rows, wmid_ref, kb_ref, put(1), first)
        return carry

    lax.fori_loop(0, MEMBERS // BATCH, middle, 0)
    for l, mask in enumerate((8, 4, 2, 1)):
        spread_kinds(kt_ref, kb_ref, l + 1)

        def read(n, l=l):
            return s_ref[(l + 1) % 2, n]

        def read_turned(n, l=l):
            return t_ref[(l + 1) % 2, n]

        def last(n, value, turned):
            out_ref[n] = value

        write = last if l == 3 else put(l % 2)
        level(read, read_turned, write, perm_ref[l], w_ref.at[l], kb_ref, mask, perm_ref[4] if l == 3 else None)


VMEM = pl.BlockSpec(memory_space=pltpu.VMEM)
SMEM = pl.BlockSpec(memory_space=pltpu.SMEM)
LIMIT = 40 * 1024 * 1024


def call(kernel, name, out_shape, in_specs, scratch=(), flops=0, count=0):
    many = isinstance(out_shape, tuple)
    return pl.pallas_call(
        kernel,
        out_shape=out_shape,
        in_specs=in_specs,
        out_specs=(VMEM,) * len(out_shape) if many else VMEM,
        scratch_shapes=list(scratch),
        compiler_params=pltpu.CompilerParams(vmem_limit_bytes=LIMIT),
        cost_estimate=pl.CostEstimate(flops=flops, bytes_accessed=count, transcendentals=0),
        name=name,
    )


def on_device(coefficients, src_blocks, mid_blocks, obs_blocks, block_ids, partner_perm, owner_order):
    a = lax.axis_index("gx")
    b = lax.axis_index("gy") // 2
    place = jnp.stack([b, a ^ b]).astype(jnp.int32)
    ordered = jnp.asarray(np.eye(CLUSTERS)[:, ORDER], BF)
    order = jnp.asarray(ORDER[None], F32)

    def shape(*dims):
        return jax.ShapeDtypeStruct(dims, BF)

    x = call(pack_kernel, "pack", shape(MEMBERS, CLUSTERS + EXTRA, LANES), [VMEM] * 4, count=2**21)(
        coefficients[0, 0], block_ids[0, 0], owner_order[0], ordered
    )
    x = lax.all_to_all(x, AXES, split_axis=0, concat_axis=0, tiled=True, axis_index_groups=SRC_GROUPS)
    square, wide = (CLUSTERS, CLUSTERS), (2, 8 * HALF, 4 * HALF)
    src_perm, obs_perm, src_w, obs_w, mid_w = call(
        table_kernel,
        "tables",
        (shape(4, *square), shape(5, *square), shape(4, *wide), shape(4, *wide), shape(2, 4 * HALF, 4 * HALF)),
        [VMEM] * 6,
        flops=10**9,
        count=2**24,
    )(src_blocks, mid_blocks, obs_blocks, partner_perm, ordered, order)

    ids = pltpu.VMEM((LANES, MEMBERS * IDS), F32)
    state = pltpu.VMEM((2, MEMBERS, CLUSTERS, LANES), BF)
    kinds = pltpu.VMEM((3, MEMBERS, CLUSTERS, LANES), BF)
    mid = call(
        source_kernel,
        "source_levels",
        shape(NA, (MEMBERS + 1) * EXTRA, LANES),
        [SMEM, VMEM, VMEM, VMEM],
        (ids, kinds, state, state, pltpu.VMEM((MEMBERS * CLUSTERS, LANES), F32)),
    )(place, x, src_perm, src_w)
    mid = lax.all_to_all(mid, AXES, split_axis=0, concat_axis=0, tiled=True, axis_index_groups=MID_GROUPS)
    done = call(
        observation_kernel,
        "observation_levels",
        shape(MEMBERS, CLUSTERS, LANES),
        [SMEM, VMEM, VMEM, VMEM, VMEM],
        (ids, kinds, state, state),
    )(place, mid, obs_perm, obs_w, mid_w)
    out = lax.all_to_all(
        done.reshape(MEMBERS * CLUSTERS, LANES),
        AXES,
        split_axis=0,
        concat_axis=1,
        tiled=True,
        axis_index_groups=OBS_GROUPS,
    )
    return out.reshape(1, 1, CLUSTERS, MEMBERS * LANES)


def solution(mesh):
    in_specs = (
        P("gy", "gx", None, None),
        P(),
        P(),
        P(),
        P("gy", "gx", None, None),
        P(),
        P("gy", "gx", None),
    )
    out_specs = P("gy", "gx", None, None)
    return jax.shard_map(on_device, mesh=mesh, in_specs=in_specs, out_specs=out_specs, check_vma=False)
```

```python
import jax
import jax.numpy as jnp
from jax import lax
from jax.experimental import pallas as pl
from jax.experimental.pallas import tpu as pltpu
from jax.sharding import PartitionSpec as P

NA = 8
MEMBERS = 16
CLUSTERS = 256
LANES = 128
HALF = 64
IDS = 16
EXTRA = 2 * IDS
AXES = ("gx", "gy")
BF = jnp.bfloat16
F32 = jnp.float32


def number(a, b, c):
    return 16 * a + 2 * b + c


SRC_GROUPS = [[number((t // 2) ^ b, b, t % 2) for t in range(MEMBERS)] for b in range(NA)]
MID_GROUPS = [[number(a, r ^ a, c) for a in range(NA)] for r in range(NA) for c in range(2)]
OBS_GROUPS = [[number(a, (t // 2) ^ a, t % 2) for t in range(MEMBERS)] for a in range(NA)]


def order_of(row):
    b, q, r, c = row >> 5, (row >> 4) & 1, (row >> 1) & 7, row & 1
    return ((r ^ b) * 16 + b * 2 + c) * 2 + q


def ordered_matrix():
    position = lax.broadcasted_iota(jnp.int32, (CLUSTERS, CLUSTERS), 0)
    row = lax.broadcasted_iota(jnp.int32, (CLUSTERS, CLUSTERS), 1)
    return jnp.where(position == order_of(row), 1.0, 0.0).astype(BF)


def pack_kernel(coef_ref, ids_ref, send_ref, out_ref, all_ref, one_ref, extra_ref, sems):
    small = [pltpu.make_async_copy(ids_ref, all_ref, sems.at[0]), pltpu.make_async_copy(send_ref, one_ref, sems.at[1])]
    slices = [
        pltpu.make_async_copy(
            coef_ref.at[:, pl.ds(t * LANES, LANES)], out_ref.at[t, pl.ds(0, CLUSTERS), :], sems.at[2 + t]
        )
        for t in range(MEMBERS)
    ]
    for copy in small + slices:
        copy.start()
    sort = ordered_matrix()
    for copy in small:
        copy.wait()
    ids = [all_ref[l].astype(F32) for l in range(9)]
    pad = jnp.zeros((3, CLUSTERS), F32)
    source = jnp.concatenate(ids[:4] + [one_ref[...].astype(F32), pad], axis=0)
    ordered = jnp.dot(jnp.concatenate(ids[:8], axis=0).astype(BF), sort, preferred_element_type=F32)
    other = jnp.concatenate([ordered[4:8], ids[8], pad], axis=0)
    extra = jnp.concatenate([source[:, :LANES], source[:, LANES:], other[:, :LANES], other[:, LANES:]], axis=0)
    extra_ref[...] = extra.astype(BF)
    below = [
        pltpu.make_async_copy(
            extra_ref, out_ref.at[t, pl.ds(CLUSTERS, EXTRA), :], sems.at[2 + MEMBERS + t]
        )
        for t in range(MEMBERS)
    ]
    for copy in below:
        copy.start()
    for copy in below + slices:
        copy.wait()


def unpack_kernel(x_ref, out_ref, sems):
    copies = [
        pltpu.make_async_copy(x_ref.at[t], out_ref.at[:, pl.ds(t * LANES, LANES)], sems.at[t]) for t in range(MEMBERS)
    ]
    for copy in copies:
        copy.start()
    for copy in copies:
        copy.wait()


def turned_weights(block, parts, lows):
    rows = []
    for low in lows:
        each = [(4 * high + low, part) for high in range(4) for part in parts]
        top = [(block(k, p, 0), -block(k, p, 1)) for k, p in each]
        bottom = [(block(k, p, 1), block(k, p, 0)) for k, p in each]
        rows += [jnp.concatenate([piece for pair in half for piece in pair], axis=1) for half in (top, bottom)]
    return jnp.concatenate(rows, axis=0).T.astype(BF)


FORMS = (((0, 1), (0, 1, 2, 3)), ((1, 0), (1, 0, 3, 2)))


def table_kernel(
    src_ref, mid_ref, obs_ref, perm_ref,
    src_perm_ref, obs_perm_ref, src_w_ref, obs_w_ref, mid_w_ref,
):
    perm = perm_ref[...].astype(F32)
    moved = jnp.dot(perm.astype(BF), ordered_matrix(), preferred_element_type=F32)
    turned = jnp.concatenate([perm, moved, jnp.zeros((LANES - 16, CLUSTERS), F32)], axis=0).T
    shape = (CLUSTERS, CLUSTERS)
    count = lax.broadcasted_iota(jnp.int32, shape, 1).astype(F32)
    order = order_of(lax.broadcasted_iota(jnp.int32, shape, 1)).astype(F32)

    def match(column, against):
        return jnp.where(jnp.broadcast_to(column, shape) == against, 1.0, 0.0).astype(BF)

    for l in range(4):
        src_perm_ref[l] = match(turned[:, l : l + 1], count)
        at = 12 + l if l < 3 else 7
        obs_perm_ref[l] = match(turned[:, at : at + 1], order)
    obs_perm_ref[4] = match(lax.broadcasted_iota(jnp.int32, shape, 0).astype(F32), order)

    def weights(l, carry):
        for form, (parts, lows) in enumerate(FORMS):
            src_w_ref[l, form] = turned_weights(lambda k, p, i: src_ref[l, k, p, i].astype(F32), parts, lows)
            obs_w_ref[l, form] = turned_weights(lambda k, p, i: obs_ref[l, k, p, i].astype(F32), parts, lows)
        return carry

    lax.fori_loop(0, 4, weights, 0)
    for form, (_, lows) in enumerate(FORMS):
        mid_w_ref[form] = turned_weights(lambda k, p, i: mid_ref[k, i].astype(F32), (0,), lows)


def coded(kinds):
    high = jnp.floor(kinds * 0.25)
    low = kinds - 4.0 * high
    second = jnp.floor(low * 0.5)
    return (high + 1.0 + 8.0 * (low - 2.0 * second)) * (1.0 - 2.0 * second)


def spread_kinds(kt_ref, kb_ref, row):
    for m in range(MEMBERS):
        for half in range(2):
            col = m * IDS + 8 * half + row
            kinds = jnp.broadcast_to(kt_ref[:, col : col + 1], (LANES, LANES))
            kb_ref[m, half * LANES : (half + 1) * LANES, :] = kinds.astype(BF)


def high_of(code):
    size = jnp.maximum(code, -code)
    return jnp.where(size >= 8.0, size - 8.0, size)


def odd_of(code):
    return jnp.maximum(code, -code) >= 8.0


def first_side():
    return lax.broadcasted_iota(jnp.int32, (CLUSTERS, LANES), 1).astype(F32).astype(BF) < HALF


def other_side(x):
    return pltpu.roll(x, HALF, 1)


def expand(x, high):
    zero = jnp.zeros_like(x)
    return jnp.concatenate([jnp.where(high == float(j + 1), x, zero) for j in range(4)], axis=1)


def expand_halves(x, high, first):
    zero = jnp.zeros_like(x)
    parts = []
    for j in (0, 2):
        parts.append(jnp.where(first, jnp.where(high == float(j + 1), x, zero), jnp.where(high == float(j + 2), x, zero)))
    return jnp.concatenate(parts, axis=1)


def multiply(ms, rows, weights, kb_ref, write, first):
    prods = [
        jnp.dot(jnp.concatenate([r[side] for r in rows], axis=0), weights[side], preferred_element_type=F32)
        for side in range(2)
    ]
    for k, m in enumerate(ms):
        second, odd = kb_ref[m] < 0.0, odd_of(kb_ref[m])
        at = slice(k * CLUSTERS, (k + 1) * CLUSTERS)
        one, two = [jnp.where(second, p[at, LANES:].astype(BF), p[at, :LANES].astype(BF)) for p in prods]
        kept = jnp.where(jnp.logical_xor(first, odd), one, two)
        turned = other_side(kept)
        write(m, jnp.where(odd, turned, kept), jnp.where(odd, kept, turned))


BATCH = 8


def level(read, read_turned, write, perm, weights, kb_ref, mask, own_perm=None):
    def body(i, carry):
        first = first_side()
        ms = [BATCH * i + k for k in range(BATCH)]
        far = jnp.concatenate([read_turned(m ^ mask) for m in ms], axis=1)
        far = jnp.dot(perm, far, preferred_element_type=F32).astype(BF)
        own = [read(m) for m in ms]
        if own_perm is not None:
            own = jnp.dot(own_perm, jnp.concatenate(own, axis=1), preferred_element_type=F32).astype(BF)
            own = [own[:, k * LANES : (k + 1) * LANES] for k in range(BATCH)]
        rows = []
        for k, m in enumerate(ms):
            x, y, high = own[k], far[:, k * LANES : (k + 1) * LANES], high_of(kb_ref[m])
            rows.append((expand(jnp.where(first, x, y), high), expand(jnp.where(first, y, x), high)))
        multiply(ms, rows, weights, kb_ref, write, first)
        return carry

    lax.fori_loop(0, MEMBERS // BATCH, body, 0)


def source_kernel(place_ref, x_ref, perm_ref, w_ref, out_ref, kt_ref, kb_ref, s_ref, t_ref, f_ref):
    b = place_ref[0]
    ids = x_ref[:, CLUSTERS : CLUSTERS + IDS, :].reshape(MEMBERS * IDS, LANES).astype(F32).T
    kt_ref[0] = ids
    kt_ref[1] = coded(ids)
    for l, mask in enumerate((2, 4, 8, 1)):
        spread_kinds(kt_ref.at[1], kb_ref, l)

        def read(m, l=l):
            return x_ref[m, :CLUSTERS, :] if l == 0 else s_ref[(l - 1) % 2, m]

        def read_turned(m, l=l):
            return other_side(x_ref[m, :CLUSTERS, :]) if l == 0 else t_ref[(l - 1) % 2, m]

        def write(m, value, turned, l=l):
            s_ref[l % 2, m] = value
            t_ref[l % 2, m] = turned

        level(read, read_turned, write, perm_ref[l], w_ref.at[l], kb_ref, mask)
    lane = lax.broadcasted_iota(jnp.int32, (LANES, LANES), 1).astype(F32)
    for m in range(MEMBERS):
        picks = []
        for half in range(2):
            col = m * IDS + 8 * half + 4
            at = jnp.broadcast_to(kt_ref[0, :, col : col + 1], (LANES, LANES))
            picks.append(
                jnp.concatenate([(at == lane).astype(F32), (at == lane + LANES).astype(F32)], axis=1).astype(BF)
            )
        sent = jnp.dot(jnp.concatenate(picks, axis=0), s_ref[1, m], preferred_element_type=F32)
        f_ref[m * CLUSTERS : (m + 1) * CLUSTERS, :] = sent
    for h in range(NA):
        for n in range(MEMBERS):
            slot = (h * MEMBERS + (n ^ (2 * h))) * 2
            parts = [
                f_ref[pl.ds(m0 * CLUSTERS + slot + q, 8, stride=CLUSTERS), :] for q in range(2) for m0 in (0, 8)
            ]
            out_ref[h, n * EXTRA : (n + 1) * EXTRA, :] = jnp.concatenate(parts, axis=0).astype(BF)
        for c in range(2):
            at = MEMBERS * EXTRA + c * IDS
            out_ref[h, at : at + IDS, :] = x_ref[(h ^ b) * 2 + c, CLUSTERS + IDS :, :]


def observation_kernel(place_ref, r_ref, perm_ref, w_ref, wmid_ref, out_ref, kt_ref, kb_ref, s_ref, t_ref):
    b, diag = place_ref[0], place_ref[1]
    ids = [r_ref[(n // 2) ^ b, pl.ds(MEMBERS * EXTRA + (n % 2) * IDS, IDS), :] for n in range(MEMBERS)]
    kt_ref[1] = coded(jnp.concatenate(ids, axis=0).astype(F32).T)
    spread_kinds(kt_ref.at[1], kb_ref, 0)

    def put(slot):
        def write(n, value, turned):
            s_ref[slot, n] = value
            t_ref[slot, n] = turned

        return write

    def middle(i, carry):
        first = first_side()
        ns = [BATCH * i + k for k in range(BATCH)]
        rows = []
        for n in ns:
            at = pl.ds(pl.multiple_of(n * EXTRA, EXTRA), EXTRA)
            x = jnp.concatenate([r_ref[j ^ diag, at, :] for j in range(NA)], axis=0)
            turned, high = other_side(x), high_of(kb_ref[n])
            one, two = jnp.where(first, x, turned), jnp.where(first, turned, x)
            rows.append((expand_halves(one, high, first), expand_halves(two, high, first)))
        multiply(ns, rows, wmid_ref, kb_ref, put(1), first)
        return carry

    lax.fori_loop(0, MEMBERS // BATCH, middle, 0)
    for l, mask in enumerate((8, 4, 2, 1)):
        spread_kinds(kt_ref.at[1], kb_ref, l + 1)

        def read(n, l=l):
            return s_ref[(l + 1) % 2, n]

        def read_turned(n, l=l):
            return t_ref[(l + 1) % 2, n]

        def last(n, value, turned):
            out_ref[n] = value

        write = last if l == 3 else put(l % 2)
        level(read, read_turned, write, perm_ref[l], w_ref.at[l], kb_ref, mask, perm_ref[4] if l == 3 else None)


VMEM = pl.BlockSpec(memory_space=pltpu.VMEM)
SMEM = pl.BlockSpec(memory_space=pltpu.SMEM)
HBM = pl.BlockSpec(memory_space=pltpu.HBM)
LIMIT = 24 * 1024 * 1024
TABLES = 16 * 1024 * 1024
SMALL = 4 * 1024 * 1024


def call(kernel, name, out_shape, in_specs, scratch=(), out_spec=None, limit=None, flops=0, count=0):
    many = isinstance(out_shape, tuple)
    spec = VMEM if out_spec is None else out_spec
    return pl.pallas_call(
        kernel,
        out_shape=out_shape,
        in_specs=in_specs,
        out_specs=(spec,) * len(out_shape) if many else spec,
        scratch_shapes=list(scratch),
        compiler_params=pltpu.CompilerParams(vmem_limit_bytes=LIMIT if limit is None else limit),
        cost_estimate=pl.CostEstimate(flops=flops, bytes_accessed=count, transcendentals=0),
        name=name,
    )


def on_device(coefficients, src_blocks, mid_blocks, obs_blocks, block_ids, partner_perm, owner_order):
    a = lax.axis_index("gx")
    b = lax.axis_index("gy") // 2
    place = jnp.stack([b, a ^ b]).astype(jnp.int32)

    def shape(*dims):
        return jax.ShapeDtypeStruct(dims, BF)

    x = call(
        pack_kernel,
        "pack",
        shape(MEMBERS, CLUSTERS + EXTRA, LANES),
        [HBM] * 3,
        (
            pltpu.VMEM((9, 1, CLUSTERS), jnp.int32),
            pltpu.VMEM((1, CLUSTERS), jnp.int32),
            pltpu.VMEM((EXTRA, LANES), BF),
            pltpu.SemaphoreType.DMA((2 + 2 * MEMBERS,)),
        ),
        out_spec=HBM,
        limit=SMALL,
        count=2**21,
    )(coefficients[0, 0], block_ids[0, 0].T[:, None, :], owner_order[0])
    x = lax.all_to_all(x, AXES, split_axis=0, concat_axis=0, tiled=True, axis_index_groups=SRC_GROUPS)
    square, wide = (CLUSTERS, CLUSTERS), (2, 8 * HALF, 4 * HALF)
    src_perm, obs_perm, src_w, obs_w, mid_w = call(
        table_kernel,
        "tables",
        (shape(4, *square), shape(5, *square), shape(4, *wide), shape(4, *wide), shape(2, 4 * HALF, 4 * HALF)),
        [VMEM] * 4,
        limit=TABLES,
        flops=10**9,
        count=2**24,
    )(src_blocks, mid_blocks, obs_blocks, partner_perm)

    ids = pltpu.VMEM((2, LANES, MEMBERS * IDS), F32)
    kinds = pltpu.VMEM((MEMBERS, CLUSTERS, LANES), BF)
    state = pltpu.VMEM((2, MEMBERS, CLUSTERS, LANES), BF)
    mid = call(
        source_kernel,
        "source_levels",
        shape(NA, (MEMBERS + 1) * EXTRA, LANES),
        [SMEM, VMEM, VMEM, VMEM],
        (ids, kinds, state, state, pltpu.VMEM((MEMBERS * CLUSTERS, LANES), F32)),
    )(place, x, src_perm, src_w)
    mid = lax.all_to_all(mid, AXES, split_axis=0, concat_axis=0, tiled=True, axis_index_groups=MID_GROUPS)
    done = call(
        observation_kernel,
        "observation_levels",
        shape(MEMBERS, CLUSTERS, LANES),
        [SMEM, VMEM, VMEM, VMEM, VMEM],
        (ids, kinds, state, state),
    )(place, mid, obs_perm, obs_w, mid_w)
    out = lax.all_to_all(done, AXES, split_axis=0, concat_axis=0, tiled=True, axis_index_groups=OBS_GROUPS)
    out = call(
        unpack_kernel,
        "unpack",
        shape(CLUSTERS, MEMBERS * LANES),
        [pl.BlockSpec(memory_space=pl.ANY)],
        (pltpu.SemaphoreType.DMA((MEMBERS,)),),
        out_spec=HBM,
        limit=SMALL,
        count=2**21,
    )(out)
    return out.reshape(1, 1, CLUSTERS, MEMBERS * LANES)


def solution(mesh):
    in_specs = (
        P("gy", "gx", None, None),
        P(),
        P(),
        P(),
        P("gy", "gx", None, None),
        P(),
        P("gy", "gx", None),
    )
    out_specs = P("gy", "gx", None, None)
    return jax.shard_map(on_device, mesh=mesh, in_specs=in_specs, out_specs=out_specs, check_vma=False)
```

```python
import jax
import jax.numpy as jnp
from jax import lax
from jax.experimental import pallas as pl
from jax.experimental.pallas import tpu as pltpu
from jax.sharding import PartitionSpec as P

NA = 8
MEMBERS = 16
CLUSTERS = 256
LANES = 128
HALF = 64
IDS = 16
EXTRA = 2 * IDS
AXES = ("gx", "gy")
BF = jnp.bfloat16
F32 = jnp.float32


def number(a, b, c):
    return 16 * a + 2 * b + c


SRC_GROUPS = [[number((t // 2) ^ b, b, t % 2) for t in range(MEMBERS)] for b in range(NA)]
MID_GROUPS = [[number(a, r ^ a, c) for a in range(NA)] for r in range(NA) for c in range(2)]
OBS_GROUPS = [[number(a, (t // 2) ^ a, t % 2) for t in range(MEMBERS)] for a in range(NA)]


def order_of(row):
    b, q, r, c = row >> 5, (row >> 4) & 1, (row >> 1) & 7, row & 1
    return ((r ^ b) * 16 + b * 2 + c) * 2 + q


def ordered_matrix():
    position = lax.broadcasted_iota(jnp.int32, (CLUSTERS, CLUSTERS), 0)
    row = lax.broadcasted_iota(jnp.int32, (CLUSTERS, CLUSTERS), 1)
    return jnp.where(position == order_of(row), 1.0, 0.0).astype(BF)


def pack_kernel(coef_ref, ids_ref, send_ref, out_ref, all_ref, one_ref, extra_ref, sems):
    small = [pltpu.make_async_copy(ids_ref, all_ref, sems.at[0]), pltpu.make_async_copy(send_ref, one_ref, sems.at[1])]
    slices = [
        pltpu.make_async_copy(
            coef_ref.at[:, pl.ds(t * LANES, LANES)], out_ref.at[t, pl.ds(0, CLUSTERS), :], sems.at[2 + t]
        )
        for t in range(MEMBERS)
    ]
    for copy in small + slices:
        copy.start()
    sort = ordered_matrix()
    for copy in small:
        copy.wait()
    ids = [all_ref[l].astype(F32) for l in range(9)]
    pad = jnp.zeros((3, CLUSTERS), F32)
    source = jnp.concatenate(ids[:4] + [one_ref[...].astype(F32), pad], axis=0)
    ordered = jnp.dot(jnp.concatenate(ids[:8], axis=0).astype(BF), sort, preferred_element_type=F32)
    other = jnp.concatenate([ordered[4:8], ids[8], pad], axis=0)
    extra = jnp.concatenate([source[:, :LANES], source[:, LANES:], other[:, :LANES], other[:, LANES:]], axis=0)
    extra_ref[...] = extra.astype(BF)
    below = [
        pltpu.make_async_copy(
            extra_ref, out_ref.at[t, pl.ds(CLUSTERS, EXTRA), :], sems.at[2 + MEMBERS + t]
        )
        for t in range(MEMBERS)
    ]
    for copy in below:
        copy.start()
    for copy in below + slices:
        copy.wait()


def unpack_kernel(x_ref, out_ref, sems):
    copies = [
        pltpu.make_async_copy(x_ref.at[t], out_ref.at[:, pl.ds(t * LANES, LANES)], sems.at[t]) for t in range(MEMBERS)
    ]
    for copy in copies:
        copy.start()
    for copy in copies:
        copy.wait()


def turned_weights(block, parts, lows):
    rows = []
    for low in lows:
        each = [(4 * high + low, part) for high in range(4) for part in parts]
        top = [(block(k, p, 0), -block(k, p, 1)) for k, p in each]
        bottom = [(block(k, p, 1), block(k, p, 0)) for k, p in each]
        rows += [jnp.concatenate([piece for pair in half for piece in pair], axis=1) for half in (top, bottom)]
    return jnp.concatenate(rows, axis=0).T.astype(BF)


FORMS = (((0, 1), (0, 1, 2, 3)), ((1, 0), (1, 0, 3, 2)))


def table_kernel(
    src_ref, mid_ref, obs_ref, perm_ref,
    src_perm_ref, obs_perm_ref, src_w_ref, obs_w_ref, mid_w_ref,
):
    perm = perm_ref[...].astype(F32)
    moved = jnp.dot(perm.astype(BF), ordered_matrix(), preferred_element_type=F32)
    turned = jnp.concatenate([perm, moved, jnp.zeros((LANES - 16, CLUSTERS), F32)], axis=0).T
    shape = (CLUSTERS, CLUSTERS)
    count = lax.broadcasted_iota(jnp.int32, shape, 1).astype(F32)
    order = order_of(lax.broadcasted_iota(jnp.int32, shape, 1)).astype(F32)

    def match(column, against):
        return jnp.where(jnp.broadcast_to(column, shape) == against, 1.0, 0.0).astype(BF)

    for l in range(4):
        src_perm_ref[l] = match(turned[:, l : l + 1], count)
        at = 12 + l if l < 3 else 7
        obs_perm_ref[l] = match(turned[:, at : at + 1], order)
    obs_perm_ref[4] = match(lax.broadcasted_iota(jnp.int32, shape, 0).astype(F32), order)

    def weights(l, carry):
        for form, (parts, lows) in enumerate(FORMS):
            src_w_ref[l, form] = turned_weights(lambda k, p, i: src_ref[l, k, p, i].astype(F32), parts, lows)
            obs_w_ref[l, form] = turned_weights(lambda k, p, i: obs_ref[l, k, p, i].astype(F32), parts, lows)
        return carry

    lax.fori_loop(0, 4, weights, 0)
    for form, (_, lows) in enumerate(FORMS):
        mid_w_ref[form] = turned_weights(lambda k, p, i: mid_ref[k, i].astype(F32), (0,), lows)


def coded(kinds):
    high = jnp.floor(kinds * 0.25)
    low = kinds - 4.0 * high
    second = jnp.floor(low * 0.5)
    return (high + 1.0 + 8.0 * (low - 2.0 * second)) * (1.0 - 2.0 * second)


def spread_kinds(kt_ref, kb_ref, row):
    for m in range(MEMBERS):
        for half in range(2):
            col = m * IDS + 8 * half + row
            kinds = jnp.broadcast_to(kt_ref[:, col : col + 1], (LANES, LANES))
            kb_ref[m, half * LANES : (half + 1) * LANES, :] = kinds


def high_of(code):
    size = jnp.maximum(code, -code)
    return jnp.where(size >= 8.0, size - 8.0, size)


def odd_of(code):
    return jnp.maximum(code, -code) >= 8.0


def first_side():
    return lax.broadcasted_iota(jnp.int32, (CLUSTERS, LANES), 1).astype(F32).astype(BF) < HALF


def other_side(x):
    return pltpu.roll(x, HALF, 1)


def expand(x, high):
    zero = jnp.zeros_like(x)
    return jnp.concatenate([jnp.where(high == float(j + 1), x, zero) for j in range(4)], axis=1)


def expand_halves(x, high, first):
    zero = jnp.zeros_like(x)
    parts = []
    for j in (0, 2):
        parts.append(jnp.where(first, jnp.where(high == float(j + 1), x, zero), jnp.where(high == float(j + 2), x, zero)))
    return jnp.concatenate(parts, axis=1)


def multiply(ms, rows, weights, kb_ref, write, first):
    kept_sides = []
    for side in range(2):
        prod = jnp.dot(jnp.concatenate([r[side]() for r in rows], axis=0), weights[side], preferred_element_type=F32)
        each = []
        for k, m in enumerate(ms):
            at = slice(k * CLUSTERS, (k + 1) * CLUSTERS)
            each.append(jnp.where(kb_ref[m] < 0.0, prod[at, LANES:], prod[at, :LANES]).astype(BF))
        kept_sides.append(each)
    for k, m in enumerate(ms):
        odd = odd_of(kb_ref[m].astype(BF))
        one, two = kept_sides[0][k], kept_sides[1][k]
        kept = jnp.where(jnp.logical_xor(first, odd), one, two)
        turned = other_side(kept)
        write(m, jnp.where(odd, turned, kept), jnp.where(odd, kept, turned))


BATCH = 16


def level(read, read_turned, write, perm, weights, kb_ref, mask, own_perm=None):
    def body(i, carry):
        first = first_side()
        ms = [BATCH * i + k for k in range(BATCH)]
        far = jnp.concatenate([read_turned(m ^ mask) for m in ms], axis=1)
        far = jnp.dot(perm, far, preferred_element_type=F32).astype(BF)
        own = [read(m) for m in ms]
        if own_perm is not None:
            own = jnp.dot(own_perm, jnp.concatenate(own, axis=1), preferred_element_type=F32).astype(BF)
            own = [own[:, k * LANES : (k + 1) * LANES] for k in range(BATCH)]
        rows = []
        for k, m in enumerate(ms):
            x, y, high = own[k], far[:, k * LANES : (k + 1) * LANES], high_of(kb_ref[m].astype(BF))
            rows.append((lambda x=x, y=y, high=high: expand(jnp.where(first, x, y), high), lambda x=x, y=y, high=high: expand(jnp.where(first, y, x), high)))
        multiply(ms, rows, weights, kb_ref, write, first)
        return carry

    lax.fori_loop(0, MEMBERS // BATCH, body, 0)


def source_kernel(place_ref, x_ref, perm_ref, w_ref, out_ref, kt_ref, kb_ref, s_ref, t_ref, f_ref):
    b = place_ref[0]
    ids = x_ref[:, CLUSTERS : CLUSTERS + IDS, :].reshape(MEMBERS * IDS, LANES).astype(F32).T
    kt_ref[0] = ids
    kt_ref[1] = coded(ids)
    for l, mask in enumerate((2, 4, 8, 1)):
        spread_kinds(kt_ref.at[1], kb_ref, l)

        def read(m, l=l):
            return x_ref[m, :CLUSTERS, :] if l == 0 else s_ref[(l - 1) % 2, m]

        def read_turned(m, l=l):
            return other_side(x_ref[m, :CLUSTERS, :]) if l == 0 else t_ref[(l - 1) % 2, m]

        def write(m, value, turned, l=l):
            s_ref[l % 2, m] = value
            t_ref[l % 2, m] = turned

        level(read, read_turned, write, perm_ref[l], w_ref.at[l], kb_ref, mask)
    lane = lax.broadcasted_iota(jnp.int32, (LANES, LANES), 1).astype(F32)
    for m in range(MEMBERS):
        picks = []
        for half in range(2):
            col = m * IDS + 8 * half + 4
            at = jnp.broadcast_to(kt_ref[0, :, col : col + 1], (LANES, LANES))
            picks.append(
                jnp.concatenate([(at == lane).astype(F32), (at == lane + LANES).astype(F32)], axis=1).astype(BF)
            )
        sent = jnp.dot(jnp.concatenate(picks, axis=0), s_ref[1, m], preferred_element_type=F32)
        f_ref[m * CLUSTERS : (m + 1) * CLUSTERS, :] = sent
    for h in range(NA):
        for n in range(MEMBERS):
            slot = (h * MEMBERS + (n ^ (2 * h))) * 2
            parts = [
                f_ref[pl.ds(m0 * CLUSTERS + slot + q, 8, stride=CLUSTERS), :] for q in range(2) for m0 in (0, 8)
            ]
            out_ref[h, n * EXTRA : (n + 1) * EXTRA, :] = jnp.concatenate(parts, axis=0).astype(BF)
        for c in range(2):
            at = MEMBERS * EXTRA + c * IDS
            out_ref[h, at : at + IDS, :] = x_ref[(h ^ b) * 2 + c, CLUSTERS + IDS :, :]


def observation_kernel(place_ref, r_ref, perm_ref, w_ref, wmid_ref, out_ref, kt_ref, kb_ref, s_ref, t_ref):
    b, diag = place_ref[0], place_ref[1]
    ids = [r_ref[(n // 2) ^ b, pl.ds(MEMBERS * EXTRA + (n % 2) * IDS, IDS), :] for n in range(MEMBERS)]
    kt_ref[1] = coded(jnp.concatenate(ids, axis=0).astype(F32).T)
    spread_kinds(kt_ref.at[1], kb_ref, 0)

    def put(slot):
        def write(n, value, turned):
            s_ref[slot, n] = value
            t_ref[slot, n] = turned

        return write

    def middle(i, carry):
        first = first_side()
        ns = [BATCH * i + k for k in range(BATCH)]
        rows = []
        for n in ns:
            at = pl.ds(pl.multiple_of(n * EXTRA, EXTRA), EXTRA)
            x = jnp.concatenate([r_ref[j ^ diag, at, :] for j in range(NA)], axis=0)
            turned, high = other_side(x), high_of(kb_ref[n].astype(BF))
            one, two = jnp.where(first, x, turned), jnp.where(first, turned, x)
            rows.append((lambda one=one, high=high: expand_halves(one, high, first), lambda two=two, high=high: expand_halves(two, high, first)))
        multiply(ns, rows, wmid_ref, kb_ref, put(1), first)
        return carry

    lax.fori_loop(0, MEMBERS // BATCH, middle, 0)
    for l, mask in enumerate((8, 4, 2, 1)):
        spread_kinds(kt_ref.at[1], kb_ref, l + 1)

        def read(n, l=l):
            return s_ref[(l + 1) % 2, n]

        def read_turned(n, l=l):
            return t_ref[(l + 1) % 2, n]

        def last(n, value, turned):
            out_ref[n] = value

        write = last if l == 3 else put(l % 2)
        level(read, read_turned, write, perm_ref[l], w_ref.at[l], kb_ref, mask, perm_ref[4] if l == 3 else None)


VMEM = pl.BlockSpec(memory_space=pltpu.VMEM)
SMEM = pl.BlockSpec(memory_space=pltpu.SMEM)
HBM = pl.BlockSpec(memory_space=pltpu.HBM)
LIMIT = 24 * 1024 * 1024
TABLES = 16 * 1024 * 1024
SMALL = 4 * 1024 * 1024


def call(kernel, name, out_shape, in_specs, scratch=(), out_spec=None, limit=None, flops=0, count=0):
    many = isinstance(out_shape, tuple)
    spec = VMEM if out_spec is None else out_spec
    return pl.pallas_call(
        kernel,
        out_shape=out_shape,
        in_specs=in_specs,
        out_specs=(spec,) * len(out_shape) if many else spec,
        scratch_shapes=list(scratch),
        compiler_params=pltpu.CompilerParams(vmem_limit_bytes=LIMIT if limit is None else limit),
        cost_estimate=pl.CostEstimate(flops=flops, bytes_accessed=count, transcendentals=0),
        name=name,
    )


def on_device(coefficients, src_blocks, mid_blocks, obs_blocks, block_ids, partner_perm, owner_order):
    a = lax.axis_index("gx")
    b = lax.axis_index("gy") // 2
    place = jnp.stack([b, a ^ b]).astype(jnp.int32)

    def shape(*dims):
        return jax.ShapeDtypeStruct(dims, BF)

    x = call(
        pack_kernel,
        "pack",
        shape(MEMBERS, CLUSTERS + EXTRA, LANES),
        [HBM] * 3,
        (
            pltpu.VMEM((9, 1, CLUSTERS), jnp.int32),
            pltpu.VMEM((1, CLUSTERS), jnp.int32),
            pltpu.VMEM((EXTRA, LANES), BF),
            pltpu.SemaphoreType.DMA((2 + 2 * MEMBERS,)),
        ),
        out_spec=HBM,
        limit=SMALL,
        count=2**21,
    )(coefficients[0, 0], lax.transpose(block_ids, (0, 3, 1, 2))[0], owner_order[0])
    x = lax.all_to_all(x, AXES, split_axis=0, concat_axis=0, tiled=True, axis_index_groups=SRC_GROUPS)
    square, wide = (CLUSTERS, CLUSTERS), (2, 8 * HALF, 4 * HALF)
    src_perm, obs_perm, src_w, obs_w, mid_w = call(
        table_kernel,
        "tables",
        (shape(4, *square), shape(5, *square), shape(4, *wide), shape(4, *wide), shape(2, 4 * HALF, 4 * HALF)),
        [VMEM] * 4,
        limit=TABLES,
        flops=10**9,
        count=2**24,
    )(src_blocks, mid_blocks, obs_blocks, partner_perm)

    ids = pltpu.VMEM((2, LANES, MEMBERS * IDS), F32)
    kinds = pltpu.VMEM((MEMBERS, CLUSTERS, LANES), F32)
    state = pltpu.VMEM((2, MEMBERS, CLUSTERS, LANES), BF)
    mid = call(
        source_kernel,
        "source_levels",
        shape(NA, (MEMBERS + 1) * EXTRA, LANES),
        [SMEM, VMEM, VMEM, VMEM],
        (ids, kinds, state, state, pltpu.VMEM((MEMBERS * CLUSTERS, LANES), F32)),
    )(place, x, src_perm, src_w)
    mid = lax.all_to_all(mid, AXES, split_axis=0, concat_axis=0, tiled=True, axis_index_groups=MID_GROUPS)
    done = call(
        observation_kernel,
        "observation_levels",
        shape(MEMBERS, CLUSTERS, LANES),
        [SMEM, VMEM, VMEM, VMEM, VMEM],
        (ids, kinds, state, state),
    )(place, mid, obs_perm, obs_w, mid_w)
    out = lax.all_to_all(done, AXES, split_axis=0, concat_axis=0, tiled=True, axis_index_groups=OBS_GROUPS)
    out = call(
        unpack_kernel,
        "unpack",
        shape(CLUSTERS, MEMBERS * LANES),
        [pl.BlockSpec(memory_space=pl.ANY)],
        (pltpu.SemaphoreType.DMA((MEMBERS,)),),
        out_spec=HBM,
        limit=SMALL,
        count=2**21,
    )(out)
    return out.reshape(1, 1, CLUSTERS, MEMBERS * LANES)


def solution(mesh):
    in_specs = (
        P("gy", "gx", None, None),
        P(),
        P(),
        P(),
        P("gy", "gx", None, None),
        P(),
        P("gy", "gx", None),
    )
    out_specs = P("gy", "gx", None, None)
    return jax.shard_map(on_device, mesh=mesh, in_specs=in_specs, out_specs=out_specs, check_vma=False)
```

```python
import jax
import jax.numpy as jnp
from jax import lax
from jax.experimental import pallas as pl
from jax.experimental.pallas import tpu as pltpu
from jax.sharding import PartitionSpec as P

NA = 8
MEMBERS = 16
CLUSTERS = 256
LANES = 128
HALF = 64
IDS = 16
EXTRA = 2 * IDS
AXES = ("gx", "gy")
BF = jnp.bfloat16
F32 = jnp.float32


def number(a, b, c):
    return 16 * a + 2 * b + c


SRC_GROUPS = [[number((t // 2) ^ b, b, t % 2) for t in range(MEMBERS)] for b in range(NA)]
MID_GROUPS = [[number(a, r ^ a, c) for a in range(NA)] for r in range(NA) for c in range(2)]
OBS_GROUPS = [[number(a, (t // 2) ^ a, t % 2) for t in range(MEMBERS)] for a in range(NA)]


def order_of(row):
    b, q, r, c = row >> 5, (row >> 4) & 1, (row >> 1) & 7, row & 1
    return ((r ^ b) * 16 + b * 2 + c) * 2 + q


def ordered_matrix():
    position = lax.broadcasted_iota(jnp.int32, (CLUSTERS, CLUSTERS), 0)
    row = lax.broadcasted_iota(jnp.int32, (CLUSTERS, CLUSTERS), 1)
    return jnp.where(position == order_of(row), 1.0, 0.0).astype(BF)


def pack_kernel(coef_ref, ids_ref, send_ref, out_ref, all_ref, one_ref, extra_ref, held_ref, sems):
    small = [pltpu.make_async_copy(ids_ref, all_ref, sems.at[0]), pltpu.make_async_copy(send_ref, one_ref, sems.at[1])]
    width = MEMBERS * LANES // PIECES
    fetched = [
        pltpu.make_async_copy(
            coef_ref.at[:, pl.ds(i * width, width)], held_ref.at[:, pl.ds(i * width, width)], sems.at[2 + 2 * MEMBERS + i]
        )
        for i in range(PIECES)
    ]
    slices = [
        pltpu.make_async_copy(
            held_ref.at[:, pl.ds(t * LANES, LANES)], out_ref.at[t, pl.ds(0, CLUSTERS), :], sems.at[2 + t]
        )
        for t in range(MEMBERS)
    ]
    for copy in small + fetched:
        copy.start()
    for i in range(PIECES):
        fetched[i].wait()
        for copy in slices[i * (MEMBERS // PIECES) : (i + 1) * (MEMBERS // PIECES)]:
            copy.start()
    sort = ordered_matrix()
    for copy in small:
        copy.wait()
    ids = [all_ref[l].astype(F32) for l in range(9)]
    pad = jnp.zeros((3, CLUSTERS), F32)
    source = jnp.concatenate(ids[:4] + [one_ref[...].astype(F32), pad], axis=0)
    ordered = jnp.dot(jnp.concatenate(ids[:8], axis=0).astype(BF), sort, preferred_element_type=F32)
    other = jnp.concatenate([ordered[4:8], ids[8], pad], axis=0)
    extra = jnp.concatenate([source[:, :LANES], source[:, LANES:], other[:, :LANES], other[:, LANES:]], axis=0)
    extra_ref[...] = extra.astype(BF)
    below = [
        pltpu.make_async_copy(
            extra_ref, out_ref.at[t, pl.ds(CLUSTERS, EXTRA), :], sems.at[2 + MEMBERS + t]
        )
        for t in range(MEMBERS)
    ]
    for copy in below:
        copy.start()
    for copy in below + slices:
        copy.wait()


def unpack_kernel(x_ref, out_ref, sems):
    copies = [
        pltpu.make_async_copy(x_ref.at[t], out_ref.at[:, pl.ds(t * LANES, LANES)], sems.at[t]) for t in range(MEMBERS)
    ]
    for copy in copies:
        copy.start()
    for copy in copies:
        copy.wait()


def turned_weights(block, parts, lows):
    rows = []
    for low in lows:
        each = [(4 * high + low, part) for high in range(4) for part in parts]
        top = [(block(k, p, 0), -block(k, p, 1)) for k, p in each]
        bottom = [(block(k, p, 1), block(k, p, 0)) for k, p in each]
        rows += [jnp.concatenate([piece for pair in half for piece in pair], axis=1) for half in (top, bottom)]
    return jnp.concatenate(rows, axis=0).T.astype(BF)


FORMS = (((0, 1), (0, 1, 2, 3)), ((1, 0), (1, 0, 3, 2)))


def table_kernel(
    src_ref, mid_ref, obs_ref, perm_ref,
    src_perm_ref, obs_perm_ref, src_w_ref, obs_w_ref, mid_w_ref,
):
    perm = perm_ref[...].astype(F32)
    moved = jnp.dot(perm.astype(BF), ordered_matrix(), preferred_element_type=F32)
    turned = jnp.concatenate([perm, moved, jnp.zeros((LANES - 16, CLUSTERS), F32)], axis=0).T
    shape = (CLUSTERS, CLUSTERS)
    count = lax.broadcasted_iota(jnp.int32, shape, 1).astype(F32)
    order = order_of(lax.broadcasted_iota(jnp.int32, shape, 1)).astype(F32)

    def match(column, against):
        return jnp.where(jnp.broadcast_to(column, shape) == against, 1.0, 0.0).astype(BF)

    for l in range(4):
        src_perm_ref[l] = match(turned[:, l : l + 1], count)
        at = 12 + l if l < 3 else 7
        obs_perm_ref[l] = match(turned[:, at : at + 1], order)
    obs_perm_ref[4] = match(lax.broadcasted_iota(jnp.int32, shape, 0).astype(F32), order)

    def weights(l, carry):
        for form, (parts, lows) in enumerate(FORMS):
            src_w_ref[l, form] = turned_weights(lambda k, p, i: src_ref[l, k, p, i].astype(F32), parts, lows)
            obs_w_ref[l, form] = turned_weights(lambda k, p, i: obs_ref[l, k, p, i].astype(F32), parts, lows)
        return carry

    lax.fori_loop(0, 4, weights, 0)
    for form, (_, lows) in enumerate(FORMS):
        mid_w_ref[form] = turned_weights(lambda k, p, i: mid_ref[k, i].astype(F32), (0,), lows)


def coded(kinds):
    high = jnp.floor(kinds * 0.25)
    low = kinds - 4.0 * high
    second = jnp.floor(low * 0.5)
    return (high + 1.0 + 8.0 * (low - 2.0 * second)) * (1.0 - 2.0 * second)


def spread_kinds(kt_ref, kb_ref, row):
    for m in range(MEMBERS):
        for half in range(2):
            col = m * IDS + 8 * half + row
            kinds = jnp.broadcast_to(kt_ref[:, col : col + 1], (LANES, LANES))
            kb_ref[m, half * LANES : (half + 1) * LANES, :] = kinds


def high_of(code):
    size = jnp.maximum(code, -code)
    return jnp.where(size >= 8.0, size - 8.0, size)


def odd_of(code):
    return jnp.maximum(code, -code) >= 8.0


def first_side():
    return lax.broadcasted_iota(jnp.int32, (CLUSTERS, LANES), 1).astype(F32).astype(BF) < HALF


def other_side(x):
    return pltpu.roll(x, HALF, 1)


def expand(x, high):
    zero = jnp.zeros_like(x)
    return jnp.concatenate([jnp.where(high == float(j + 1), x, zero) for j in range(4)], axis=1)


def expand_halves(x, high, first):
    zero = jnp.zeros_like(x)
    parts = []
    for j in (0, 2):
        parts.append(jnp.where(first, jnp.where(high == float(j + 1), x, zero), jnp.where(high == float(j + 2), x, zero)))
    return jnp.concatenate(parts, axis=1)


def multiply(ms, rows, weights, kb_ref, write, first):
    kept_sides = []
    for side in range(2):
        prod = jnp.dot(jnp.concatenate([r[side]() for r in rows], axis=0), weights[side], preferred_element_type=F32)
        each = []
        for k, m in enumerate(ms):
            at = slice(k * CLUSTERS, (k + 1) * CLUSTERS)
            each.append(jnp.where(kb_ref[m] < 0.0, prod[at, LANES:], prod[at, :LANES]).astype(BF))
        kept_sides.append(each)
    for k, m in enumerate(ms):
        odd = odd_of(kb_ref[m].astype(BF))
        one, two = kept_sides[0][k], kept_sides[1][k]
        kept = jnp.where(jnp.logical_xor(first, odd), one, two)
        turned = other_side(kept)
        write(m, jnp.where(odd, turned, kept), jnp.where(odd, kept, turned))


BATCH = 16


def level(read, read_turned, write, perm, weights, kb_ref, mask, own_perm=None):
    def body(i, carry):
        first = first_side()
        ms = [BATCH * i + k for k in range(BATCH)]
        far = jnp.concatenate([read_turned(m ^ mask) for m in ms], axis=1)
        far = jnp.dot(perm, far, preferred_element_type=F32).astype(BF)
        own = [read(m) for m in ms]
        if own_perm is not None:
            own = jnp.dot(own_perm, jnp.concatenate(own, axis=1), preferred_element_type=F32).astype(BF)
            own = [own[:, k * LANES : (k + 1) * LANES] for k in range(BATCH)]
        rows = []
        for k, m in enumerate(ms):
            x, y, high = own[k], far[:, k * LANES : (k + 1) * LANES], high_of(kb_ref[m].astype(BF))
            rows.append((lambda x=x, y=y, high=high: expand(jnp.where(first, x, y), high), lambda x=x, y=y, high=high: expand(jnp.where(first, y, x), high)))
        multiply(ms, rows, weights, kb_ref, write, first)
        return carry

    lax.fori_loop(0, MEMBERS // BATCH, body, 0)


def source_kernel(place_ref, x_ref, perm_ref, w_ref, out_ref, kt_ref, kb_ref, s_ref, t_ref, f_ref):
    b = place_ref[0]
    ids = x_ref[:, CLUSTERS : CLUSTERS + IDS, :].reshape(MEMBERS * IDS, LANES).astype(F32).T
    kt_ref[0] = ids
    kt_ref[1] = coded(ids)
    for l, mask in enumerate((2, 4, 8, 1)):
        spread_kinds(kt_ref.at[1], kb_ref, l)

        def read(m, l=l):
            return x_ref[m, :CLUSTERS, :] if l == 0 else s_ref[(l - 1) % 2, m]

        def read_turned(m, l=l):
            return other_side(x_ref[m, :CLUSTERS, :]) if l == 0 else t_ref[(l - 1) % 2, m]

        def write(m, value, turned, l=l):
            s_ref[l % 2, m] = value
            if l < 3:
                t_ref[l % 2, m] = turned

        level(read, read_turned, write, perm_ref[l], w_ref.at[l], kb_ref, mask)
    lane = lax.broadcasted_iota(jnp.int32, (LANES, LANES), 1).astype(F32)
    for m in range(MEMBERS):
        picks = []
        for half in range(2):
            col = m * IDS + 8 * half + 4
            at = jnp.broadcast_to(kt_ref[0, :, col : col + 1], (LANES, LANES))
            picks.append(
                jnp.concatenate([(at == lane).astype(F32), (at == lane + LANES).astype(F32)], axis=1).astype(BF)
            )
        sent = jnp.dot(jnp.concatenate(picks, axis=0), s_ref[1, m], preferred_element_type=F32)
        f_ref[m * CLUSTERS : (m + 1) * CLUSTERS, :] = sent
    for h in range(NA):
        for n in range(MEMBERS):
            slot = (h * MEMBERS + (n ^ (2 * h))) * 2
            parts = [
                f_ref[pl.ds(m0 * CLUSTERS + slot + q, 8, stride=CLUSTERS), :] for q in range(2) for m0 in (0, 8)
            ]
            out_ref[h, n * EXTRA : (n + 1) * EXTRA, :] = jnp.concatenate(parts, axis=0).astype(BF)
        for c in range(2):
            at = MEMBERS * EXTRA + c * IDS
            out_ref[h, at : at + IDS, :] = x_ref[(h ^ b) * 2 + c, CLUSTERS + IDS :, :]


def observation_kernel(place_ref, r_ref, perm_ref, w_ref, wmid_ref, out_ref, kt_ref, kb_ref, s_ref, t_ref):
    b, diag = place_ref[0], place_ref[1]
    ids = [r_ref[(n // 2) ^ b, pl.ds(MEMBERS * EXTRA + (n % 2) * IDS, IDS), :] for n in range(MEMBERS)]
    kt_ref[1] = coded(jnp.concatenate(ids, axis=0).astype(F32).T)
    spread_kinds(kt_ref.at[1], kb_ref, 0)

    def put(slot):
        def write(n, value, turned):
            s_ref[slot, n] = value
            t_ref[slot, n] = turned

        return write

    def middle(i, carry):
        first = first_side()
        ns = [BATCH * i + k for k in range(BATCH)]
        rows = []
        for n in ns:
            at = pl.ds(pl.multiple_of(n * EXTRA, EXTRA), EXTRA)
            x = jnp.concatenate([r_ref[j ^ diag, at, :] for j in range(NA)], axis=0)
            turned, high = other_side(x), high_of(kb_ref[n].astype(BF))
            one, two = jnp.where(first, x, turned), jnp.where(first, turned, x)
            rows.append((lambda one=one, high=high: expand_halves(one, high, first), lambda two=two, high=high: expand_halves(two, high, first)))
        multiply(ns, rows, wmid_ref, kb_ref, put(1), first)
        return carry

    lax.fori_loop(0, MEMBERS // BATCH, middle, 0)
    for l, mask in enumerate((8, 4, 2, 1)):
        spread_kinds(kt_ref.at[1], kb_ref, l + 1)

        def read(n, l=l):
            return s_ref[(l + 1) % 2, n]

        def read_turned(n, l=l):
            return t_ref[(l + 1) % 2, n]

        def last(n, value, turned):
            out_ref[n] = value

        write = last if l == 3 else put(l % 2)
        level(read, read_turned, write, perm_ref[l], w_ref.at[l], kb_ref, mask, perm_ref[4] if l == 3 else None)


VMEM = pl.BlockSpec(memory_space=pltpu.VMEM)
SMEM = pl.BlockSpec(memory_space=pltpu.SMEM)
HBM = pl.BlockSpec(memory_space=pltpu.HBM)
LIMIT = 24 * 1024 * 1024
TABLES = 16 * 1024 * 1024
SMALL = 4 * 1024 * 1024
LARGE = 60 * 1024 * 1024
PIECES = 4


def call(kernel, name, out_shape, in_specs, scratch=(), out_spec=None, limit=None, flops=0, count=0):
    many = isinstance(out_shape, tuple)
    spec = VMEM if out_spec is None else out_spec
    return pl.pallas_call(
        kernel,
        out_shape=out_shape,
        in_specs=in_specs,
        out_specs=(spec,) * len(out_shape) if many else spec,
        scratch_shapes=list(scratch),
        compiler_params=pltpu.CompilerParams(vmem_limit_bytes=LIMIT if limit is None else limit),
        cost_estimate=pl.CostEstimate(flops=flops, bytes_accessed=count, transcendentals=0),
        name=name,
    )


def on_device(coefficients, src_blocks, mid_blocks, obs_blocks, block_ids, partner_perm, owner_order):
    a = lax.axis_index("gx")
    b = lax.axis_index("gy") // 2
    place = jnp.stack([b, a ^ b]).astype(jnp.int32)

    def shape(*dims):
        return jax.ShapeDtypeStruct(dims, BF)

    x = call(
        pack_kernel,
        "pack",
        shape(MEMBERS, CLUSTERS + EXTRA, LANES),
        [HBM] * 3,
        (
            pltpu.VMEM((9, 1, CLUSTERS), jnp.int32),
            pltpu.VMEM((1, CLUSTERS), jnp.int32),
            pltpu.VMEM((EXTRA, LANES), BF),
            pltpu.VMEM((CLUSTERS, MEMBERS * LANES), BF),
            pltpu.SemaphoreType.DMA((2 + 2 * MEMBERS + PIECES,)),
        ),
        out_spec=HBM,
        limit=LARGE,
        count=2**21,
    )(coefficients[0, 0], lax.transpose(block_ids, (0, 3, 1, 2))[0], owner_order[0])
    x = lax.all_to_all(x, AXES, split_axis=0, concat_axis=0, tiled=True, axis_index_groups=SRC_GROUPS)
    square, wide = (CLUSTERS, CLUSTERS), (2, 8 * HALF, 4 * HALF)
    src_perm, obs_perm, src_w, obs_w, mid_w = call(
        table_kernel,
        "tables",
        (shape(4, *square), shape(5, *square), shape(4, *wide), shape(4, *wide), shape(2, 4 * HALF, 4 * HALF)),
        [VMEM] * 4,
        limit=TABLES,
        flops=10**9,
        count=2**24,
    )(src_blocks, mid_blocks, obs_blocks, partner_perm)

    ids = pltpu.VMEM((2, LANES, MEMBERS * IDS), F32)
    kinds = pltpu.VMEM((MEMBERS, CLUSTERS, LANES), F32)
    state = pltpu.VMEM((2, MEMBERS, CLUSTERS, LANES), BF)
    mid = call(
        source_kernel,
        "source_levels",
        shape(NA, (MEMBERS + 1) * EXTRA, LANES),
        [SMEM, VMEM, VMEM, VMEM],
        (ids, kinds, state, state, pltpu.VMEM((MEMBERS * CLUSTERS, LANES), F32)),
    )(place, x, src_perm, src_w)
    mid = lax.all_to_all(mid, AXES, split_axis=0, concat_axis=0, tiled=True, axis_index_groups=MID_GROUPS)
    done = call(
        observation_kernel,
        "observation_levels",
        shape(MEMBERS, CLUSTERS, LANES),
        [SMEM, VMEM, VMEM, VMEM, VMEM],
        (ids, kinds, state, state),
    )(place, mid, obs_perm, obs_w, mid_w)
    out = lax.all_to_all(done, AXES, split_axis=0, concat_axis=0, tiled=True, axis_index_groups=OBS_GROUPS)
    out = call(
        unpack_kernel,
        "unpack",
        shape(CLUSTERS, MEMBERS * LANES),
        [pl.BlockSpec(memory_space=pl.ANY)],
        (pltpu.SemaphoreType.DMA((MEMBERS,)),),
        out_spec=HBM,
        limit=SMALL,
        count=2**21,
    )(out)
    return out.reshape(1, 1, CLUSTERS, MEMBERS * LANES)


def solution(mesh):
    in_specs = (
        P("gy", "gx", None, None),
        P(),
        P(),
        P(),
        P("gy", "gx", None, None),
        P(),
        P("gy", "gx", None),
    )
    out_specs = P("gy", "gx", None, None)
    return jax.shard_map(on_device, mesh=mesh, in_specs=in_specs, out_specs=out_specs, check_vma=False)
```

```python
import jax
import jax.numpy as jnp
from jax import lax
from jax.experimental import pallas as pl
from jax.experimental.pallas import tpu as pltpu
from jax.sharding import PartitionSpec as P

NA = 8
MEMBERS = 16
CLUSTERS = 256
LANES = 128
HALF = 64
IDS = 16
EXTRA = 2 * IDS
AXES = ("gx", "gy")
BF = jnp.bfloat16
F32 = jnp.float32


def number(a, b, c):
    return 16 * a + 2 * b + c


SRC_GROUPS = [[number((t // 2) ^ b, b, t % 2) for t in range(MEMBERS)] for b in range(NA)]
MID_GROUPS = [[number(a, r ^ a, c) for a in range(NA)] for r in range(NA) for c in range(2)]
OBS_GROUPS = [[number(a, (t // 2) ^ a, t % 2) for t in range(MEMBERS)] for a in range(NA)]


def order_of(row):
    b, q, r, c = row >> 5, (row >> 4) & 1, (row >> 1) & 7, row & 1
    return ((r ^ b) * 16 + b * 2 + c) * 2 + q


def ordered_matrix():
    position = lax.broadcasted_iota(jnp.int32, (CLUSTERS, CLUSTERS), 0)
    row = lax.broadcasted_iota(jnp.int32, (CLUSTERS, CLUSTERS), 1)
    return jnp.where(position == order_of(row), 1.0, 0.0).astype(BF)


def pack_kernel(coef_ref, ids_ref, send_ref, out_ref, all_ref, one_ref, extra_ref, held_ref, sems):
    small = [pltpu.make_async_copy(ids_ref, all_ref, sems.at[0]), pltpu.make_async_copy(send_ref, one_ref, sems.at[1])]
    width = MEMBERS * LANES // PIECES
    fetched = [
        pltpu.make_async_copy(
            coef_ref.at[:, pl.ds(i * width, width)], held_ref.at[:, pl.ds(i * width, width)], sems.at[2 + 2 * MEMBERS + i]
        )
        for i in range(PIECES)
    ]
    slices = [
        pltpu.make_async_copy(
            held_ref.at[:, pl.ds(t * LANES, LANES)], out_ref.at[t, pl.ds(0, CLUSTERS), :], sems.at[2 + t]
        )
        for t in range(MEMBERS)
    ]
    for copy in small + fetched:
        copy.start()
    for i in range(PIECES):
        fetched[i].wait()
        for copy in slices[i * (MEMBERS // PIECES) : (i + 1) * (MEMBERS // PIECES)]:
            copy.start()
    sort = ordered_matrix()
    for copy in small:
        copy.wait()
    ids = [all_ref[l].astype(F32) for l in range(9)]
    pad = jnp.zeros((3, CLUSTERS), F32)
    source = jnp.concatenate(ids[:4] + [one_ref[...].astype(F32), pad], axis=0)
    ordered = jnp.dot(jnp.concatenate(ids[:8], axis=0).astype(BF), sort, preferred_element_type=F32)
    other = jnp.concatenate([ordered[4:8], ids[8], pad], axis=0)
    extra = jnp.concatenate([source[:, :LANES], source[:, LANES:], other[:, :LANES], other[:, LANES:]], axis=0)
    extra_ref[...] = extra.astype(BF)
    below = [
        pltpu.make_async_copy(
            extra_ref, out_ref.at[t, pl.ds(CLUSTERS, EXTRA), :], sems.at[2 + MEMBERS + t]
        )
        for t in range(MEMBERS)
    ]
    for copy in below:
        copy.start()
    for copy in below + slices:
        copy.wait()


def unpack_kernel(x_ref, out_ref, sems):
    copies = [
        pltpu.make_async_copy(x_ref.at[t], out_ref.at[:, pl.ds(t * LANES, LANES)], sems.at[t]) for t in range(MEMBERS)
    ]
    for copy in copies:
        copy.start()
    for copy in copies:
        copy.wait()


def turned_weights(block, parts, lows):
    rows = []
    for low in lows:
        each = [(4 * high + low, part) for high in range(4) for part in parts]
        top = [(block(k, p, 0), -block(k, p, 1)) for k, p in each]
        bottom = [(block(k, p, 1), block(k, p, 0)) for k, p in each]
        rows += [jnp.concatenate([piece for pair in half for piece in pair], axis=1) for half in (top, bottom)]
    return jnp.concatenate(rows, axis=0).T.astype(BF)


FORMS = (((0, 1), (0, 1, 2, 3)), ((1, 0), (1, 0, 3, 2)))


def table_kernel(
    src_ref, mid_ref, obs_ref, perm_ref,
    src_perm_ref, obs_perm_ref, src_w_ref, obs_w_ref, mid_w_ref,
):
    perm = perm_ref[...].astype(F32)
    moved = jnp.dot(perm.astype(BF), ordered_matrix(), preferred_element_type=F32)
    turned = jnp.concatenate([perm, moved, jnp.zeros((LANES - 16, CLUSTERS), F32)], axis=0).T
    shape = (CLUSTERS, CLUSTERS)
    count = lax.broadcasted_iota(jnp.int32, shape, 1).astype(F32)
    order = order_of(lax.broadcasted_iota(jnp.int32, shape, 1)).astype(F32)

    def match(column, against):
        return jnp.where(jnp.broadcast_to(column, shape) == against, 1.0, 0.0).astype(BF)

    for l in range(4):
        src_perm_ref[l] = match(turned[:, l : l + 1], count)
        at = 12 + l if l < 3 else 7
        obs_perm_ref[l] = match(turned[:, at : at + 1], order)
    obs_perm_ref[4] = match(lax.broadcasted_iota(jnp.int32, shape, 0).astype(F32), order)

    def weights(l, carry):
        for form, (parts, lows) in enumerate(FORMS):
            src_w_ref[l, form] = turned_weights(lambda k, p, i: src_ref[l, k, p, i].astype(F32), parts, lows)
            obs_w_ref[l, form] = turned_weights(lambda k, p, i: obs_ref[l, k, p, i].astype(F32), parts, lows)
        return carry

    lax.fori_loop(0, 4, weights, 0)
    for form, (_, lows) in enumerate(FORMS):
        mid_w_ref[form] = turned_weights(lambda k, p, i: mid_ref[k, i].astype(F32), (0,), lows)


def coded(kinds):
    high = jnp.floor(kinds * 0.25)
    low = kinds - 4.0 * high
    second = jnp.floor(low * 0.5)
    return (high + 1.0 + 8.0 * (low - 2.0 * second)) * (1.0 - 2.0 * second)


def spread_kinds(kt_ref, kb_ref, row):
    for m in range(MEMBERS):
        for half in range(2):
            col = m * IDS + 8 * half + row
            kinds = jnp.broadcast_to(kt_ref[:, col : col + 1], (LANES, LANES))
            kb_ref[m, half * LANES : (half + 1) * LANES, :] = kinds


def high_of(code):
    size = jnp.maximum(code, -code)
    return jnp.where(size >= 8.0, size - 8.0, size)


def odd_of(code):
    return jnp.maximum(code, -code) >= 8.0


def first_side():
    return lax.broadcasted_iota(jnp.int32, (CLUSTERS, LANES), 1).astype(F32).astype(BF) < HALF


def other_side(x):
    return pltpu.roll(x, HALF, 1)


def expand(x, high):
    zero = jnp.zeros_like(x)
    return jnp.concatenate([jnp.where(high == float(j + 1), x, zero) for j in range(4)], axis=1)


def expand_halves(x, high, first):
    zero = jnp.zeros_like(x)
    parts = []
    for j in (0, 2):
        parts.append(jnp.where(first, jnp.where(high == float(j + 1), x, zero), jnp.where(high == float(j + 2), x, zero)))
    return jnp.concatenate(parts, axis=1)


def multiply(ms, rows, weights, kb_ref, write, first):
    kept_sides = []
    for side in range(2):
        prod = jnp.dot(jnp.concatenate([r[side]() for r in rows], axis=0), weights[side], preferred_element_type=F32)
        each = []
        for k, m in enumerate(ms):
            at = slice(k * CLUSTERS, (k + 1) * CLUSTERS)
            each.append(jnp.where(kb_ref[m] < 0.0, prod[at, LANES:], prod[at, :LANES]).astype(BF))
        kept_sides.append(each)
    for k, m in enumerate(ms):
        odd = odd_of(kb_ref[m].astype(BF))
        one, two = kept_sides[0][k], kept_sides[1][k]
        kept = jnp.where(jnp.logical_xor(first, odd), one, two)
        turned = other_side(kept)
        write(m, jnp.where(odd, turned, kept), jnp.where(odd, kept, turned))


BATCH = 16


def level(read, read_turned, write, perm, weights, kb_ref, mask, own_perm=None):
    def body(i, carry):
        first = first_side()
        ms = [BATCH * i + k for k in range(BATCH)]
        far = jnp.concatenate([read_turned(m ^ mask) for m in ms], axis=1)
        far = jnp.dot(perm, far, preferred_element_type=F32).astype(BF)
        own = [read(m) for m in ms]
        if own_perm is not None:
            own = jnp.dot(own_perm, jnp.concatenate(own, axis=1), preferred_element_type=F32).astype(BF)
            own = [own[:, k * LANES : (k + 1) * LANES] for k in range(BATCH)]
        rows = []
        for k, m in enumerate(ms):
            x, y, high = own[k], far[:, k * LANES : (k + 1) * LANES], high_of(kb_ref[m].astype(BF))
            rows.append((lambda x=x, y=y, high=high: expand(jnp.where(first, x, y), high), lambda x=x, y=y, high=high: expand(jnp.where(first, y, x), high)))
        multiply(ms, rows, weights, kb_ref, write, first)
        return carry

    lax.fori_loop(0, MEMBERS // BATCH, body, 0)


def source_kernel(place_ref, x_ref, far_ref, w_ref, out_ref, kt_ref, kb_ref, s_ref, t_ref, f_ref, perm_ref, sem):
    fetch = pltpu.make_async_copy(far_ref, perm_ref, sem)
    fetch.start()
    b = place_ref[0]
    ids = x_ref[:, CLUSTERS : CLUSTERS + IDS, :].reshape(MEMBERS * IDS, LANES).astype(F32).T
    kt_ref[0] = ids
    kt_ref[1] = coded(ids)
    for l, mask in enumerate((2, 4, 8, 1)):
        spread_kinds(kt_ref.at[1], kb_ref, l)
        if l == 0:
            fetch.wait()

        def read(m, l=l):
            return x_ref[m, :CLUSTERS, :] if l == 0 else s_ref[(l - 1) % 2, m]

        def read_turned(m, l=l):
            return other_side(x_ref[m, :CLUSTERS, :]) if l == 0 else t_ref[(l - 1) % 2, m]

        def write(m, value, turned, l=l):
            s_ref[l % 2, m] = value
            if l < 3:
                t_ref[l % 2, m] = turned

        level(read, read_turned, write, perm_ref[l], w_ref.at[l], kb_ref, mask)
    lane = lax.broadcasted_iota(jnp.int32, (LANES, LANES), 1).astype(F32)
    for m in range(MEMBERS):
        picks = []
        for half in range(2):
            col = m * IDS + 8 * half + 4
            at = jnp.broadcast_to(kt_ref[0, :, col : col + 1], (LANES, LANES))
            picks.append(
                jnp.concatenate([(at == lane).astype(F32), (at == lane + LANES).astype(F32)], axis=1).astype(BF)
            )
        sent = jnp.dot(jnp.concatenate(picks, axis=0), s_ref[1, m], preferred_element_type=F32)
        f_ref[m * CLUSTERS : (m + 1) * CLUSTERS, :] = sent
    for h in range(NA):
        for n in range(MEMBERS):
            slot = (h * MEMBERS + (n ^ (2 * h))) * 2
            parts = [
                f_ref[pl.ds(m0 * CLUSTERS + slot + q, 8, stride=CLUSTERS), :] for q in range(2) for m0 in (0, 8)
            ]
            out_ref[h, n * EXTRA : (n + 1) * EXTRA, :] = jnp.concatenate(parts, axis=0).astype(BF)
        for c in range(2):
            at = MEMBERS * EXTRA + c * IDS
            out_ref[h, at : at + IDS, :] = x_ref[(h ^ b) * 2 + c, CLUSTERS + IDS :, :]


def observation_kernel(place_ref, r_ref, perm_ref, w_ref, wmid_ref, out_ref, kt_ref, kb_ref, s_ref, t_ref):
    b, diag = place_ref[0], place_ref[1]
    ids = [r_ref[(n // 2) ^ b, pl.ds(MEMBERS * EXTRA + (n % 2) * IDS, IDS), :] for n in range(MEMBERS)]
    kt_ref[1] = coded(jnp.concatenate(ids, axis=0).astype(F32).T)
    spread_kinds(kt_ref.at[1], kb_ref, 0)

    def put(slot):
        def write(n, value, turned):
            s_ref[slot, n] = value
            t_ref[slot, n] = turned

        return write

    def middle(i, carry):
        first = first_side()
        ns = [BATCH * i + k for k in range(BATCH)]
        rows = []
        for n in ns:
            at = pl.ds(pl.multiple_of(n * EXTRA, EXTRA), EXTRA)
            x = jnp.concatenate([r_ref[j ^ diag, at, :] for j in range(NA)], axis=0)
            turned, high = other_side(x), high_of(kb_ref[n].astype(BF))
            one, two = jnp.where(first, x, turned), jnp.where(first, turned, x)
            rows.append((lambda one=one, high=high: expand_halves(one, high, first), lambda two=two, high=high: expand_halves(two, high, first)))
        multiply(ns, rows, wmid_ref, kb_ref, put(1), first)
        return carry

    lax.fori_loop(0, MEMBERS // BATCH, middle, 0)
    for l, mask in enumerate((8, 4, 2, 1)):
        spread_kinds(kt_ref.at[1], kb_ref, l + 1)

        def read(n, l=l):
            return s_ref[(l + 1) % 2, n]

        def read_turned(n, l=l):
            return t_ref[(l + 1) % 2, n]

        def last(n, value, turned):
            out_ref[n] = value

        write = last if l == 3 else put(l % 2)
        level(read, read_turned, write, perm_ref[l], w_ref.at[l], kb_ref, mask, perm_ref[4] if l == 3 else None)


VMEM = pl.BlockSpec(memory_space=pltpu.VMEM)
SMEM = pl.BlockSpec(memory_space=pltpu.SMEM)
HBM = pl.BlockSpec(memory_space=pltpu.HBM)
LIMIT = 24 * 1024 * 1024
TABLES = 16 * 1024 * 1024
SMALL = 4 * 1024 * 1024
LARGE = 60 * 1024 * 1024
PIECES = 4


def call(kernel, name, out_shape, in_specs, scratch=(), out_spec=None, limit=None, flops=0, count=0):
    many = isinstance(out_shape, tuple)
    spec = VMEM if out_spec is None else out_spec
    return pl.pallas_call(
        kernel,
        out_shape=out_shape,
        in_specs=in_specs,
        out_specs=(spec,) * len(out_shape) if many else spec,
        scratch_shapes=list(scratch),
        compiler_params=pltpu.CompilerParams(vmem_limit_bytes=LIMIT if limit is None else limit),
        cost_estimate=pl.CostEstimate(flops=flops, bytes_accessed=count, transcendentals=0),
        name=name,
    )


def on_device(coefficients, src_blocks, mid_blocks, obs_blocks, block_ids, partner_perm, owner_order):
    a = lax.axis_index("gx")
    b = lax.axis_index("gy") // 2
    place = jnp.stack([b, a ^ b]).astype(jnp.int32)

    def shape(*dims):
        return jax.ShapeDtypeStruct(dims, BF)

    x = call(
        pack_kernel,
        "pack",
        shape(MEMBERS, CLUSTERS + EXTRA, LANES),
        [HBM] * 3,
        (
            pltpu.VMEM((9, 1, CLUSTERS), jnp.int32),
            pltpu.VMEM((1, CLUSTERS), jnp.int32),
            pltpu.VMEM((EXTRA, LANES), BF),
            pltpu.VMEM((CLUSTERS, MEMBERS * LANES), BF),
            pltpu.SemaphoreType.DMA((2 + 2 * MEMBERS + PIECES,)),
        ),
        out_spec=HBM,
        limit=LARGE,
        count=2**21,
    )(coefficients[0, 0], lax.transpose(block_ids, (0, 3, 1, 2))[0], owner_order[0])
    x = lax.all_to_all(x, AXES, split_axis=0, concat_axis=0, tiled=True, axis_index_groups=SRC_GROUPS)
    square, wide = (CLUSTERS, CLUSTERS), (2, 8 * HALF, 4 * HALF)
    src_perm, obs_perm, src_w, obs_w, mid_w = call(
        table_kernel,
        "tables",
        (shape(4, *square), shape(5, *square), shape(4, *wide), shape(4, *wide), shape(2, 4 * HALF, 4 * HALF)),
        [VMEM] * 4,
        limit=TABLES,
        flops=10**9,
        count=2**24,
    )(src_blocks, mid_blocks, obs_blocks, partner_perm)

    ids = pltpu.VMEM((2, LANES, MEMBERS * IDS), F32)
    kinds = pltpu.VMEM((MEMBERS, CLUSTERS, LANES), F32)
    state = pltpu.VMEM((2, MEMBERS, CLUSTERS, LANES), BF)
    mid = call(
        source_kernel,
        "source_levels",
        shape(NA, (MEMBERS + 1) * EXTRA, LANES),
        [SMEM, VMEM, HBM, VMEM],
        (
            ids, kinds, state, state, pltpu.VMEM((MEMBERS * CLUSTERS, LANES), F32),
            pltpu.VMEM((4, *square), BF), pltpu.SemaphoreType.DMA(()),
        ),
    )(place, x, src_perm, src_w)
    mid = lax.all_to_all(mid, AXES, split_axis=0, concat_axis=0, tiled=True, axis_index_groups=MID_GROUPS)
    done = call(
        observation_kernel,
        "observation_levels",
        shape(MEMBERS, CLUSTERS, LANES),
        [SMEM, VMEM, VMEM, VMEM, VMEM],
        (ids, kinds, state, state),
    )(place, mid, obs_perm, obs_w, mid_w)
    out = lax.all_to_all(done, AXES, split_axis=0, concat_axis=0, tiled=True, axis_index_groups=OBS_GROUPS)
    out = call(
        unpack_kernel,
        "unpack",
        shape(CLUSTERS, MEMBERS * LANES),
        [pl.BlockSpec(memory_space=pl.ANY)],
        (pltpu.SemaphoreType.DMA((MEMBERS,)),),
        out_spec=HBM,
        limit=SMALL,
        count=2**21,
    )(out)
    return out.reshape(1, 1, CLUSTERS, MEMBERS * LANES)


def solution(mesh):
    in_specs = (
        P("gy", "gx", None, None),
        P(),
        P(),
        P(),
        P("gy", "gx", None, None),
        P(),
        P("gy", "gx", None),
    )
    out_specs = P("gy", "gx", None, None)
    return jax.shard_map(on_device, mesh=mesh, in_specs=in_specs, out_specs=out_specs, check_vma=False)
```
